512 devices in a mesh: ep: 64 (over z, y), tp: 8 (over x, core).
Axes of the slice: x: 4, y: 8, z: 8, core: 2. Of those that a mesh axis runs over, the one named last changes fastest.
Arguments:
- tokens: bfloat16 [1024, 3072], P('ep'), may hold values from -6 to 6
- expert_ids: int32 [1024, 2], P('ep'), may hold values from 0 to 7, all different within a row; in each aligned block of 16 rows (0 to 15, 16 to 31, ...) at most 6 rows name the same one
- combine: float32 [1024, 2], P('ep'), may hold values from 0.2 to 1
- grad_out: bfloat16 [1024, 3072], P('ep'), may hold values from -6 to 6
- gate_weight: bfloat16 [3072, 65536], P(None, ('ep', 'tp')), may hold values from -0.109375 to 0.109375
- up_weight: bfloat16 [3072, 65536], P(None, ('ep', 'tp')), may hold values from -0.109375 to 0.109375
- down_weight: bfloat16 [65536, 3072], P(('ep', 'tp')), may hold values from -0.0625 to 0.0625
Outputs:
- mixed: bfloat16 [1024, 3072], P('ep')
- grad_tokens: bfloat16 [1024, 3072], P('ep')
- grad_combine: float32 [1024, 2], P('ep')
- grad_gate: bfloat16 [3072, 65536], P(None, ('ep', 'tp'))
- grad_up: bfloat16 [3072, 65536], P(None, ('ep', 'tp'))
- grad_down: bfloat16 [65536, 3072], P(('ep', 'tp'))
The draws below stay inside these ranges and needn't reach their ends.
Inputs may be any that keep to these rules, and one draw needn't show every extreme that they name: `expert_ids`: each row names 2 different experts. Among the 16 rows of one index of ep no expert is named more than 6 times, a bound that some block reaches.
All inputs are finite; a program needn't handle non-finite values.
Results may differ from the reference program's by a relative error of at most 0.0057.
Values may be sent and summed in bfloat16 or wider, within the bound.
A program may use at most 128 MiB of HBM per device.

```python
import math
import jax
import jax.numpy as jnp
import numpy as np
from jax import lax

D = 3072
FF = 8192
E = 8
TOP = 2
TOK_DEV = 16
CAP = 6
TOKENS = 1024
N_EP = 64


def levels(own_key, extent, cuts, low, largest):
    loudness = 1.0
    for dim, parts in cuts:
        steps = jax.random.uniform(jax.random.fold_in(jax.random.fold_in(own_key, 6), dim), (parts,), jnp.float32, low / len(cuts), largest / len(cuts))
        loudness = loudness * jnp.repeat(jnp.exp(steps), extent[dim] // parts).reshape((-1,) + (1,) * (len(extent) - 1 - dim))
    return loudness


def assign_block(key, own, number, rows, amount, top, bound, slope):
    order = jax.random.permutation(key, amount)
    packed, ordinary = portions_of(amount, rows * top, bound, slope, True), portions_of(amount, rows * top, bound, slope, False)
    places = jnp.arange(amount)

    def named(lengths, turn):
        used = int((lengths > 0).sum())
        fixed = max(1, used // 4)
        shifted = fixed + (places - fixed + turn * (used - fixed)) % max(1, amount - fixed)
        return jnp.zeros((amount,), jnp.int32).at[order[jnp.where(places < fixed, places, shifted)]].set(jnp.asarray(lengths, jnp.int32))

    lengths = jnp.where(number % 4 == 0, named(packed, number // 4), named(ordinary, number - number // 4 - 1))
    mixed = jax.random.permutation(jax.random.fold_in(own, 3), amount)
    giver, sink = mixed[0:amount // 2 * 2:2], mixed[1:amount // 2 * 2:2]
    slack = jnp.minimum(lengths[giver] - 1, bound - lengths[sink]) // 2
    slack = jnp.where((giver == order[0]) | (sink == order[0]) | (lengths[sink] == 0), 0, jnp.maximum(slack, 0))
    shifted = jax.random.randint(jax.random.fold_in(own, 4), (amount // 2,), 0, 1 << 20) % (slack + 1)
    lengths = lengths.at[giver].add(-shifted).at[sink].add(shifted)
    items = jnp.searchsorted(jnp.cumsum(lengths), jnp.arange(rows * top), side="right").astype(jnp.int32)
    grid = items.reshape(top, rows).T
    grid = grid[jax.random.permutation(jax.random.fold_in(own, 1), rows)]
    turn = jax.random.randint(jax.random.fold_in(own, 2), (rows, 1), 0, top)
    return jnp.take_along_axis(grid, (jnp.arange(top)[None, :] + turn) % top, axis=1)


def portions_of(amount, total, most, skew, full):
    loads = [(1 << 20) // math.isqrt(standing ** skew) + 1 for standing in range(1, amount + 1)]
    largest = most if full else min(most, max(-(-total // amount), total * loads[0] // sum(loads)))
    least = 1 if total - largest >= amount - 1 else 0
    holding, surplus = [largest] + [least] * (amount - 1), total - largest - least * (amount - 1)
    while surplus > 0:
        movable = [i for i in range(1, amount) if holding[i] < largest] or [i for i in range(1, amount) if holding[i] < most]
        whole, left = sum([loads[i] for i in movable]), surplus
        for i in movable:
            more = min(most - holding[i], max(1, left * loads[i] // whole), surplus)
            holding[i] = holding[i] + more
            surplus = surplus - more
    return np.array(holding)


def scatter_about(stream_key, extent, width, bound, pieces=(), kind=jnp.bfloat16):
    entries = jax.random.normal(stream_key, extent, jnp.float32) * width
    if len(pieces) > 0:
        entries = levels(stream_key, extent, pieces, -0.22, 0.18) * entries
    return jnp.clip(entries, min=-bound, max=bound).astype(kind)


def setup_inputs(seed: int = 0) -> dict:
    splits = jax.random.split(jax.random.key(seed), 8)
    tokens = scatter_about(splits[0], (TOKENS, D), 1.0, 6.0, ((0, 64),))
    expert_ids_keys = jax.random.split(jax.random.fold_in(splits[1], 1), TOKENS // TOK_DEV)
    expert_ids_turns = jax.random.permutation(jax.random.fold_in(splits[1], 3), TOKENS // TOK_DEV)
    expert_ids = jax.vmap(lambda own, number: assign_block(jax.random.fold_in(splits[1], 2), own, number, TOK_DEV, E, TOP, CAP, 2))(expert_ids_keys, expert_ids_turns).reshape((TOKENS, TOP))
    combine = jnp.clip(0.2 + 0.8 * jax.random.uniform(splits[2], (TOKENS, TOP), jnp.float32) ** levels(splits[2], (TOKENS, TOP), ((0, 64),), -0.2, 0.2), 0.2, 1.0)
    grad_out = scatter_about(splits[3], (TOKENS, D), 1.0, 6.0, ((0, 64),))
    gate_weight = scatter_about(splits[4], (D, E * FF), D ** -0.5, 0.109375, ((1, 512),))
    up_weight = scatter_about(splits[5], (D, E * FF), D ** -0.5, 0.109375, ((1, 512),))
    down_weight = scatter_about(splits[6], (E * FF, D), FF ** -0.5, 0.0625, ((0, 512),))
    return {"tokens": tokens, "expert_ids": expert_ids, "combine": combine, "grad_out": grad_out, "gate_weight": gate_weight, "up_weight": up_weight, "down_weight": down_weight}


def expert_rows(rows_in, rows_grad, gate_part, up_part, down_part):
    gate_pre = jnp.dot(rows_in, gate_part, preferred_element_type=jnp.float32)
    up_pre = jnp.dot(rows_in, up_part, preferred_element_type=jnp.float32)
    sigmoid_gate = jax.nn.sigmoid(gate_pre)
    silu_gate = gate_pre * sigmoid_gate
    hidden = (silu_gate * up_pre).astype(jnp.bfloat16)
    partial_value = jnp.dot(hidden, down_part, preferred_element_type=jnp.float32)
    d_hidden = lax.dot_general(rows_grad, down_part, (((1,), (1,)), ((), ())), preferred_element_type=jnp.float32)
    d_gate = (d_hidden * up_pre * sigmoid_gate * (1.0 + gate_pre * (1.0 - sigmoid_gate))).astype(jnp.bfloat16)
    d_up = (d_hidden * silu_gate).astype(jnp.bfloat16)
    back_rows = lax.dot_general(d_gate, gate_part, (((1,), (1,)), ((), ())), preferred_element_type=jnp.float32)
    back_rows = back_rows + lax.dot_general(d_up, up_part, (((1,), (1,)), ((), ())), preferred_element_type=jnp.float32)
    grad_down = lax.dot_general(hidden, rows_grad, (((0,), (0,)), ((), ())), preferred_element_type=jnp.float32)
    grad_gate = lax.dot_general(rows_in, d_gate, (((0,), (0,)), ((), ())), preferred_element_type=jnp.float32)
    grad_up = lax.dot_general(rows_in, d_up, (((0,), (0,)), ((), ())), preferred_element_type=jnp.float32)
    return partial_value, back_rows, grad_gate, grad_up, grad_down


def reference(tokens, expert_ids, combine, grad_out, gate_weight, up_weight, down_weight):
    total = TOKENS * TOP
    row_count = N_EP * CAP
    flat_ids = expert_ids.reshape(total)
    owner = jnp.arange(total, dtype=jnp.int32) // TOP
    weights_flat = combine.reshape(total)
    scaled = (weights_flat[:, None] * grad_out[owner].astype(jnp.float32)).astype(jnp.bfloat16)

    def select_expert(expert):
        row_order = jnp.argsort((flat_ids != expert).astype(jnp.int32), stable=True)[:row_count].astype(jnp.int32)
        valid = flat_ids[row_order] == expert
        rows_in = jnp.where(valid[:, None], tokens[owner[row_order]], jnp.zeros((), tokens.dtype))
        rows_grad = jnp.where(valid[:, None], scaled[row_order], jnp.zeros((), scaled.dtype))
        gate_part = lax.dynamic_slice_in_dim(gate_weight, expert * FF, FF, 1)
        up_part = lax.dynamic_slice_in_dim(up_weight, expert * FF, FF, 1)
        down_part = lax.dynamic_slice_in_dim(down_weight, expert * FF, FF, 0)
        partial_value, back_rows, grad_g, grad_u, grad_d = expert_rows(rows_in, rows_grad, gate_part, up_part, down_part)
        target = jnp.where(valid, row_order, total).astype(jnp.int32)
        return partial_value, back_rows, target, grad_g.astype(jnp.bfloat16), grad_u.astype(jnp.bfloat16), grad_d.astype(jnp.bfloat16)

    partial_value, back_rows, target, grad_g, grad_u, grad_d = lax.map(select_expert, jnp.arange(E, dtype=jnp.int32))
    flat_target = target.reshape(E * row_count)
    expert_out = jnp.zeros((total + 1, D), jnp.float32).at[flat_target].add(partial_value.reshape(E * row_count, D))
    expert_out = expert_out[:total].reshape(TOKENS, TOP, D)
    back_all = jnp.zeros((total + 1, D), jnp.float32).at[flat_target].add(back_rows.reshape(E * row_count, D))
    back_all = back_all[:total].reshape(TOKENS, TOP, D)
    mixed = jnp.sum(combine[:, :, None] * expert_out, axis=1).astype(jnp.bfloat16)
    grad_combine = jnp.sum(grad_out.astype(jnp.float32)[:, None, :] * expert_out, axis=2)
    grad_tokens = jnp.sum(back_all, axis=1).astype(jnp.bfloat16)
    grad_gate = jnp.transpose(grad_g, (1, 0, 2)).reshape(D, E * FF)
    grad_up = jnp.transpose(grad_u, (1, 0, 2)).reshape(D, E * FF)
    grad_down = grad_d.reshape(E * FF, D)
    return (mixed, grad_tokens, grad_combine, grad_gate, grad_up, grad_down)
```

```python
import functools

import jax
import jax.numpy as jnp
from jax import lax
from jax.experimental import pallas as pl
from jax.experimental.pallas import tpu as pltpu
from jax.sharding import PartitionSpec as P

CAP = 6
CORES = 2
MESH = pl.DeviceIdType.MESH
F32 = jnp.float32
BF16 = jnp.bfloat16


def dot_nn(a, b):
    return jnp.dot(a, b, preferred_element_type=F32)


def dot_nt(a, b):
    return lax.dot_general(a, b, (((1,), (1,)), ((), ())), preferred_element_type=F32)


def dot_tn(a, b):
    return lax.dot_general(a, b, (((0,), (0,)), ((), ())), preferred_element_type=F32)


def kernel(
    dims,
    ids_ref, comb_ref, tok_ref, go_ref, gate_hbm, up_hbm, down_hbm,
    mixed_ref, gtok_ref, gcomb_ref, gg_hbm, gu_hbm, gd_hbm,
    xg, part, sib_out, sib_in, xs, xr, ys, yr, res,
    slab_out, slab_in, fin, fsc, pick, wgu, wd, hid, dgu, ggs, gus, gds,
    w_sem, za_s, za_r, zb_s, zb_r, gx, gy, g_send, d_send, d_recv,
    p_send, p_recv, rx_s, rx_r, ry_s, ry_r, f_s, f_r, o_sem,
):
    NX, NY, NZ, CAPA = dims
    PIECE = NZ * CAPA
    TOKB, D = tok_ref.shape
    SL = D // NX
    HS = SL // 2
    ROWS = NY * PIECE
    PER = NX * NY
    HID = wd.shape[1]

    ep, tp = lax.axis_index("ep"), lax.axis_index("tp")
    c, x = lax.rem(tp, CORES), lax.div(tp, CORES)
    y, z = lax.rem(ep, NY), lax.div(ep, NY)

    def wx(v):
        return lax.rem(v + 2 * NX, NX)

    def wy(v):
        return lax.rem(v + 2 * NY, NY)

    def at(xx, yy, zz, cc):
        return (zz * NY + yy, xx * CORES + cc)

    right, left = at(wx(x + 1), y, z, c), at(wx(x - 1), y, z, c)
    yup, ydown = at(x, wy(y + 1), z, c), at(x, wy(y - 1), z, c)
    sibling = at(x, y, z, 1 - c)
    xdev, ydev = (right, left), (yup, ydown)

    def remote(src, dst, ssem, rsem, device):
        return pltpu.make_async_remote_copy(
            src_ref=src, dst_ref=dst, send_sem=ssem, recv_sem=rsem,
            device_id=device, device_id_type=MESH,
        )

    def arrived(dst, rsem):
        remote(dst, dst, rsem, rsem, sibling).wait_recv()

    def sent(src, ssem):
        remote(src, src, ssem, ssem, sibling).wait_send()

    loads = []
    for i in range(NX):
        rows = pl.ds(i * SL, SL)
        loads.append(pltpu.make_async_copy(gate_hbm.at[rows, :], wgu.at[i, :, pl.ds(0, HID)], w_sem.at[3 * i]))
        loads.append(pltpu.make_async_copy(up_hbm.at[rows, :], wgu.at[i, :, pl.ds(HID, HID)], w_sem.at[3 * i + 1]))
        loads.append(pltpu.make_async_copy(down_hbm.at[:, rows], wd.at[i], w_sem.at[3 * i + 2]))
    for load in loads:
        load.start()

    barrier = pltpu.get_barrier_semaphore()
    peers_z = [at(x, y, lax.rem(z + d, NZ), c) for d in range(1, NZ)]
    NT = NX * CORES
    peers_t = [(ep, lax.rem(tp + d, NT)) for d in range(1, NT)]
    partners = peers_z + peers_t + [yup, ydown]
    for device in partners:
        pl.semaphore_signal(barrier, inc=1, device_id=device, device_id_type=MESH)

    lane = lax.broadcasted_iota(jnp.int32, (TOKB, NZ * 16), 1)
    expert, place = lax.shift_right_logical(lane, 4), lane & 15
    id0, id1 = ids_ref[:, 0:1], ids_ref[:, 1:2]
    is0, is1 = id0 == expert, id1 == expert
    named = jnp.where(is0 | is1, 1.0, 0.0)
    earlier = jnp.where(
        lax.broadcasted_iota(jnp.int32, (TOKB, TOKB), 0) > lax.broadcasted_iota(jnp.int32, (TOKB, TOKB), 1), 1.0, 0.0
    )
    rank = dot_nn(earlier.astype(BF16), named.astype(BF16)).astype(jnp.int32)
    hit0 = rank == place
    hit1 = (rank + CAPA == place) & (rank < CAPA)
    hit0 = hit0 & (place < CAPA)
    for g, mask in enumerate((is0 & hit0, is1 & hit0, is0 & hit1, is1 & hit1)):
        pick[g * TOKB : (g + 1) * TOKB, :] = jnp.where(mask, 1.0, 0.0).astype(BF16)

    one = jnp.ones((TOKB, 1), F32)
    w0 = jnp.where(c == 0, one, comb_ref[:, 0:1])
    w1 = jnp.where(c == 0, one, comb_ref[:, 1:2])
    span0 = pl.ds(pl.multiple_of(x * SL, 128), HS)
    span1 = pl.ds(pl.multiple_of(x * SL + HS, 128), HS)
    sources = []
    for span in (span0, span1):
        v = jnp.where(c == 0, tok_ref[:, span].astype(F32), go_ref[:, span].astype(F32))
        sources += [(v * w0).astype(BF16), (v * w1).astype(BF16)]
    slabs = dot_tn(pick[...], jnp.concatenate(sources, axis=0)).astype(BF16)
    for e in range(NZ):
        slab_out[0, e] = slabs[e * 16 : (e + 1) * 16]
    slab_in[0, z] = slab_out[0, z]

    pl.semaphore_wait(barrier, len(partners))

    def exchange_z(which, s_sem, r_sem):
        for d in range(1, NZ):
            remote(
                slab_out.at[which, lax.rem(z + d, NZ)], slab_in.at[which, z],
                s_sem.at[d], r_sem.at[d], peers_z[d - 1],
            ).start()
        for d in range(1, NZ):
            arrived(slab_in.at[which, lax.rem(z - d + NZ, NZ)], r_sem.at[d])

    exchange_z(0, za_s, za_r)

    row = lax.broadcasted_iota(jnp.int32, (PIECE, NZ * 16), 0)
    col = lax.broadcasted_iota(jnp.int32, (PIECE, NZ * 16), 1)
    block, inner = lax.shift_right_logical(col, 4), col & 15
    tidy0 = jnp.where((block * CAPA + inner == row) & (inner < CAPA), 1.0, 0.0).astype(BF16)
    tidy1 = jnp.where(
        (block * CAPA + inner - CAPA == row) & (inner >= CAPA) & (inner < 2 * CAPA), 1.0, 0.0
    ).astype(BF16)
    got = slab_in[0].reshape(NZ * 16, HS)
    mine = c * PER + x * NY + y
    xg[mine, :, 0:HS] = dot_nn(tidy0, got).astype(BF16)
    xg[mine, :, HS:SL] = dot_nn(tidy1, got).astype(BF16)

    halves = (pl.ds(0, HS), pl.ds(HS, HS))
    HX, HY = NX // 2, NY // 2

    def to_sibling(p):
        remote(xg.at[p], xg.at[p], d_send, d_recv, sibling).start()

    def send(ref, sem, device):
        remote(ref, ref, g_send, sem, device).start()

    def gather_y_then_x():
        def piece(xx, yy):
            return xx * NY + yy

        order = [0]
        for k in range(1, HY):
            order += [-k, k]
        order += [HY]

        def along_x(i):
            p = piece(x, wy(y + order[i]))
            send(xg.at[p], gx.at[0, i, 0], right)
            send(xg.at[p], gx.at[1, i, 0], left)
            to_sibling(p)

        def onward_x(i):
            yy = wy(y + order[i])
            for d, neighbour in enumerate((wx(x - 1), wx(x + 1))):
                p = piece(neighbour, yy)
                arrived(xg.at[p], gx.at[d, i, 0])
                send(xg.at[p, :, halves[d]], gx.at[d, i, 1], xdev[d])
                to_sibling(p)

        p = piece(x, y)
        send(xg.at[p], gy.at[0, 0, 0], yup)
        send(xg.at[p], gy.at[0, 1, 0], ydown)
        along_x(0)
        for k in range(1, HY + 1):
            for d in range(2):
                p = piece(x, wy(y - k if d == 0 else y + k))
                if k < HY:
                    arrived(xg.at[p], gy.at[0, d, k - 1])
                    sub = xg.at[p] if k < HY - 1 else xg.at[p, :, halves[d]]
                    send(sub, gy.at[0, d, k], ydev[d])
                else:
                    arrived(xg.at[p, :, halves[d]], gy.at[0, d, k - 1])
            if k < HY:
                along_x(2 * k - 1)
                along_x(2 * k)
                for i in [0] if k == 1 else [2 * k - 3, 2 * k - 2]:
                    onward_x(i)
            else:
                along_x(2 * k - 1)
                for i in (2 * k - 3, 2 * k - 2, 2 * k - 1):
                    onward_x(i)
        for i in range(NY):
            p = piece(wx(x + 2), wy(y + order[i]))
            for d in range(2):
                arrived(xg.at[p, :, halves[d]], gx.at[d, i, 1])
            to_sibling(p)

    def gather_x_then_y():
        def piece(xx, yy):
            return PER + xx * NY + yy

        def begin_y(j, xx):
            p = piece(xx, y)
            send(xg.at[p], gy.at[j, 0, 0], yup)
            send(xg.at[p], gy.at[j, 1, 0], ydown)
            to_sibling(p)

        xorder = [x, wx(x - 1), wx(x + 1), wx(x + 2)]
        p = piece(x, y)
        send(xg.at[p], gx.at[0, 0, 0], right)
        send(xg.at[p], gx.at[1, 0, 0], left)
        begin_y(0, x)
        for d in range(2):
            p = piece(xorder[1 + d], y)
            arrived(xg.at[p], gx.at[d, 0, 0])
            send(xg.at[p, :, halves[d]], gx.at[d, 0, 1], xdev[d])
            begin_y(1 + d, xorder[1 + d])
        p = piece(xorder[3], y)
        for d in range(2):
            arrived(xg.at[p, :, halves[d]], gx.at[d, 0, 1])
        begin_y(3, xorder[3])
        for k in range(1, HY + 1):
            for j in range(NX):
                for d in range(2):
                    p = piece(xorder[j], wy(y - k if d == 0 else y + k))
                    if k < HY:
                        arrived(xg.at[p], gy.at[j, d, k - 1])
                        sub = xg.at[p] if k < HY - 1 else xg.at[p, :, halves[d]]
                        send(sub, gy.at[j, d, k], ydev[d])
                        to_sibling(p)
                    else:
                        arrived(xg.at[p, :, halves[d]], gy.at[j, d, k - 1])
                        if d == 1:
                            to_sibling(p)

    pl.when(c == 0)(gather_y_then_x)
    pl.when(c == 1)(gather_x_then_y)
    arrived(xg.at[pl.ds((1 - c) * PER, PER)], d_recv)

    for load in loads:
        load.wait()

    def rows_of(a, i):
        return xg[a * PER + i * NY : a * PER + (i + 1) * NY].reshape(ROWS, SL)

    pre = dot_nn(rows_of(0, 0), wgu[0])
    d_hidden = dot_nt(rows_of(1, 0), wd[0])
    for i in range(1, NX):
        pre = pre + dot_nn(rows_of(0, i), wgu[i])
        d_hidden = d_hidden + dot_nt(rows_of(1, i), wd[i])
    gate_pre, up_pre = pre[:, :HID], pre[:, HID:]
    sigma = jax.nn.sigmoid(gate_pre)
    silu = gate_pre * sigma
    hid[...] = (silu * up_pre).astype(BF16)
    dgu[:, :HID] = (d_hidden * up_pre * sigma * (1.0 + gate_pre * (1.0 - sigma))).astype(BF16)
    dgu[:, HID:] = (d_hidden * silu).astype(BF16)

    def pieces(v):
        return v.reshape(NY, PIECE, SL)

    def partial_chunk(j, carry):
        xx = wx(x + 2 - j)
        span = pl.ds(xx * NY, NY)

        @pl.when(c == 0)
        def _():
            sib_out[span] = pieces(dot_nt(dgu[...], wgu[xx])).astype(BF16)
            remote(sib_out.at[span], sib_in.at[span], p_send.at[j], p_recv.at[j], sibling).start()
            part[span] = pieces(dot_nn(hid[...], wd[xx]))

        @pl.when(c == 1)
        def _():
            sib_out[span] = pieces(dot_nn(hid[...], wd[xx])).astype(BF16)
            remote(sib_out.at[span], sib_in.at[span], p_send.at[j], p_recv.at[j], sibling).start()
            part[span] = pieces(dot_nt(dgu[...], wgu[xx]))

        return carry

    lax.fori_loop(0, NX, partial_chunk, 0)

    def weight_grads(i, carry):
        rows_x = xg[pl.ds(i * NY, NY)].reshape(ROWS, SL)
        rows_g = xg[pl.ds(PER + i * NY, NY)].reshape(ROWS, SL)
        both = dot_tn(rows_x, dgu[...])
        ggs[i] = both[:, :HID].astype(BF16)
        gus[i] = both[:, HID:].astype(BF16)
        gds[i] = dot_tn(hid[...], rows_g).astype(BF16)
        return carry

    lax.fori_loop(0, NX, weight_grads, 0)
    stores = []
    for i in range(NX):
        rows = pl.ds(i * SL, SL)
        stores.append(pltpu.make_async_copy(ggs.at[i], gg_hbm.at[rows, :], o_sem.at[3 * i]))
        stores.append(pltpu.make_async_copy(gus.at[i], gu_hbm.at[rows, :], o_sem.at[3 * i + 1]))
        stores.append(pltpu.make_async_copy(gds.at[i], gd_hbm.at[:, rows], o_sem.at[3 * i + 2]))
    for store in stores:
        store.start()

    def from_sibling(j):
        arrived(sib_in.at[pl.ds(wx(x + 2 - j) * NY, NY)], p_recv.at[j])

    def own(p):
        return part[p] + sib_in[p].astype(F32)

    def reduce_x_then_y():
        def each_y(fn):
            def step(i, carry):
                fn(i)
                return carry

            lax.fori_loop(0, NY, step, 0)

        def push(d, m):
            remote(xs.at[d, m], xr.at[d, m], rx_s.at[d, m], rx_r.at[d, m], xdev[d]).start()

        from_sibling(0)
        far = wx(x + 2) * NY

        @each_y
        def _(i):
            v = own(far + i)
            xs[0, 0, i] = v[:, :HS].astype(BF16)
            xs[1, 0, i] = v[:, HS:].astype(BF16)

        push(0, 0)
        push(1, 0)
        from_sibling(1)
        from_sibling(3)
        to_r, to_l = wx(x + 1) * NY, wx(x - 1) * NY

        @each_y
        def _(i):
            v = own(to_r + i)
            part[to_r + i] = v
            xs[0, 1, i] = v[:, HS:].astype(BF16)

        push(0, 1)

        @each_y
        def _(i):
            v = own(to_l + i)
            part[to_l + i] = v
            xs[1, 1, i] = v[:, :HS].astype(BF16)

        push(1, 1)
        arrived(xr.at[0, 0], rx_r.at[0, 0])

        @each_y
        def _(i):
            xs[0, 2, i] = (part[to_r + i, :, 0:HS] + xr[0, 0, i].astype(F32)).astype(BF16)

        push(0, 2)
        arrived(xr.at[1, 0], rx_r.at[1, 0])

        @each_y
        def _(i):
            xs[1, 2, i] = (part[to_l + i, :, HS:SL] + xr[1, 0, i].astype(F32)).astype(BF16)

        push(1, 2)
        from_sibling(2)
        for m in (1, 2):
            for d in range(2):
                arrived(xr.at[d, m], rx_r.at[d, m])
        base = x * NY

        @each_y
        def _(i):
            v = own(base + i)
            part[base + i, :, 0:HS] = v[:, :HS] + xr[0, 2, i].astype(F32) + xr[1, 1, i].astype(F32)
            part[base + i, :, HS:SL] = v[:, HS:] + xr[0, 1, i].astype(F32) + xr[1, 2, i].astype(F32)

        for t in range(HY):
            for d in range(2):
                p = base + wy(y + HY - t if d == 0 else y - HY + t)
                y_step(0, d, t, part[p])
        arrived(yr.at[0, 0, HY - 1], ry_r.at[0, 0, HY - 1])
        arrived(yr.at[0, 1, HY - 1], ry_r.at[0, 1, HY - 1])
        res[x] = part[base + y] + yr[0, 0, HY - 1].astype(F32) + yr[0, 1, HY - 1].astype(F32)

    def y_step(j, d, t, v):
        out = ys.at[j, d, t]
        if t == 0:
            h = halves[d]
            out[:, h] = (v[:, :HS] if d == 0 else v[:, HS:]).astype(BF16)
            out, into = out.at[:, h], yr.at[j, d, t].at[:, h]
        elif t == 1:
            h = halves[d]
            arrived(yr.at[j, d, 0].at[:, h], ry_r.at[j, d, 0])
            came = yr[j, d, 0, :, h].astype(F32)
            lo, hi = v[:, :HS], v[:, HS:]
            lo, hi = (lo + came, hi) if d == 0 else (lo, hi + came)
            out[:, 0:HS] = lo.astype(BF16)
            out[:, HS:SL] = hi.astype(BF16)
            into = yr.at[j, d, t]
        else:
            arrived(yr.at[j, d, t - 1], ry_r.at[j, d, t - 1])
            out[...] = (v + yr[j, d, t - 1].astype(F32)).astype(BF16)
            into = yr.at[j, d, t]
        remote(out, into, ry_s.at[j, d, t], ry_r.at[j, d, t], ydev[d]).start()

    def reduce_y_then_x():
        def pair(j, t):
            xx = wx(x + 2 - j)
            for d in range(2):
                y_step(j, d, t, own(xx * NY + wy(y + HY - t if d == 0 else y - HY + t)))

        for t in range(HY):
            for j in range(NX):
                if t == 0:
                    from_sibling(j)
                pair(j, t)

        def total(j):
            xx = wx(x + 2 - j)
            for d in range(2):
                arrived(yr.at[j, d, HY - 1], ry_r.at[j, d, HY - 1])
            res[xx] = own(xx * NY + y) + yr[j, 0, HY - 1].astype(F32) + yr[j, 1, HY - 1].astype(F32)
            return xx

        def push(d, m, v):
            xs[d, m, 0] = v.astype(BF16)
            remote(xs.at[d, m, 0], xr.at[d, m, 0], rx_s.at[d, m], rx_r.at[d, m], xdev[d]).start()

        far = total(0)
        push(0, 0, res[far, :, 0:HS])
        push(1, 0, res[far, :, HS:SL])
        to_r = total(1)
        push(0, 1, res[to_r, :, HS:SL])
        to_l = total(3)
        push(1, 1, res[to_l, :, 0:HS])
        arrived(xr.at[0, 0, 0], rx_r.at[0, 0])
        push(0, 2, res[to_r, :, 0:HS] + xr[0, 0, 0].astype(F32))
        arrived(xr.at[1, 0, 0], rx_r.at[1, 0])
        push(1, 2, res[to_l, :, HS:SL] + xr[1, 0, 0].astype(F32))
        total(2)
        for m in (1, 2):
            for d in range(2):
                arrived(xr.at[d, m, 0], rx_r.at[d, m])
        res[x, :, 0:HS] = res[x, :, 0:HS] + xr[0, 2, 0].astype(F32) + xr[1, 1, 0].astype(F32)
        res[x, :, HS:SL] = res[x, :, HS:SL] + xr[0, 1, 0].astype(F32) + xr[1, 2, 0].astype(F32)

    pl.when(c == 0)(reduce_x_then_y)
    pl.when(c == 1)(reduce_y_then_x)

    done = res[x].astype(BF16)
    back = (dot_tn(tidy0, done[:, :HS]) + dot_tn(tidy1, done[:, HS:])).astype(BF16)
    for e in range(NZ):
        slab_out[1, e] = back[e * 16 : (e + 1) * 16]
    slab_in[1, z] = slab_out[1, z]
    exchange_z(1, zb_s, zb_r)
    chosen = dot_nn(pick[...], slab_in[1].reshape(NZ * 16, HS))
    c0 = jnp.where(c == 0, comb_ref[:, 0:1], one)
    c1 = jnp.where(c == 0, comb_ref[:, 1:2], one)
    scores = [jnp.zeros((TOKB, 1), F32), jnp.zeros((TOKB, 1), F32)]
    for h, span in enumerate((span0, span1)):
        first = chosen[2 * h * TOKB : (2 * h + 1) * TOKB]
        second = chosen[(2 * h + 1) * TOKB : (2 * h + 2) * TOKB]
        fin[tp, :, h * HS : (h + 1) * HS] = (c0 * first + c1 * second).astype(BF16)
        g = go_ref[:, span].astype(F32)
        scores[0] = scores[0] + jnp.sum(g * first, axis=1, keepdims=True)
        scores[1] = scores[1] + jnp.sum(g * second, axis=1, keepdims=True)
    lane = lax.broadcasted_iota(jnp.int32, (TOKB, 128), 1)
    fsc[tp] = jnp.where(lane == 0, scores[0], jnp.where(lane == 1, scores[1], 0.0))

    for d in range(1, NT):
        remote(fin.at[tp], fin.at[tp], f_s.at[0, d], f_r.at[0, d], peers_t[d - 1]).start()
        remote(fsc.at[tp], fsc.at[tp], f_s.at[1, d], f_r.at[1, d], peers_t[d - 1]).start()
    for d in range(1, NT):
        source = lax.rem(tp - d + NT, NT)
        arrived(fin.at[source], f_r.at[0, d])
        arrived(fsc.at[source], f_r.at[1, d])
    total_score = fsc[0]
    for i in range(NX):
        mixed_ref[:, i * SL : (i + 1) * SL] = fin[CORES * i]
        gtok_ref[:, i * SL : (i + 1) * SL] = fin[CORES * i + 1]
        if i:
            total_score = total_score + fsc[CORES * i]
    gcomb_ref[...] = total_score[:, 0:2]

    for store in stores:
        store.wait()
    for d in range(1, NZ):
        sent(slab_out.at[0, 0], za_s.at[d])
        sent(slab_out.at[1, 0], zb_s.at[d])
    for d in range(1, NT):
        sent(fin.at[tp], f_s.at[0, d])
        sent(fsc.at[tp], f_s.at[1, d])
    sent(xg.at[pl.ds(0, PER - 1)], g_send)
    sent(xg.at[pl.ds(c * PER, PER)], d_send)
    for j in range(NX):
        sent(sib_out.at[pl.ds(0, NY)], p_send.at[j])

    def y_sent(j):
        for d in range(2):
            sent(ys.at[j, d, 0].at[:, halves[d]], ry_s.at[j, d, 0])
            for t in range(1, HY):
                sent(ys.at[j, d, t], ry_s.at[j, d, t])

    @pl.when(c == 0)
    def _():
        for d in range(2):
            for m in range(3):
                sent(xs.at[d, m], rx_s.at[d, m])
        y_sent(0)

    @pl.when(c == 1)
    def _():
        for d in range(2):
            for m in range(3):
                sent(xs.at[d, m, 0], rx_s.at[d, m])
        for j in range(NX):
            y_sent(j)


def solution(mesh, cap=CAP, planes=8):
    NT = mesh.shape["tp"]
    NX, NZ = NT // CORES, planes
    NY = mesh.shape["ep"] // NZ

    def step(tokens, expert_ids, combine, grad_out, gate_weight, up_weight, down_weight):
        tokb, d = tokens.shape
        hidden = gate_weight.shape[1]
        sl, piece, per = d // NX, NZ * cap, NX * NY
        hs, rows, half_y = sl // 2, NY * piece, NY // 2
        dma, vmem, hbm = pltpu.SemaphoreType.DMA, pltpu.VMEM, pl.BlockSpec(memory_space=pl.ANY)
        held = pl.BlockSpec(memory_space=pltpu.VMEM)
        return pl.pallas_call(
            functools.partial(kernel, (NX, NY, NZ, cap)),
            out_shape=(
                jax.ShapeDtypeStruct((tokb, d), BF16),
                jax.ShapeDtypeStruct((tokb, d), BF16),
                jax.ShapeDtypeStruct(combine.shape, F32),
                jax.ShapeDtypeStruct(gate_weight.shape, BF16),
                jax.ShapeDtypeStruct(up_weight.shape, BF16),
                jax.ShapeDtypeStruct(down_weight.shape, BF16),
            ),
            in_specs=[held] * 4 + [hbm] * 3,
            out_specs=[held] * 3 + [hbm] * 3,
            scratch_shapes=[
                vmem((2 * per, piece, sl), BF16),
                vmem((per, piece, sl), F32),
                vmem((per, piece, sl), BF16),
                vmem((per, piece, sl), BF16),
                vmem((2, 3, NY, piece, hs), BF16),
                vmem((2, 3, NY, piece, hs), BF16),
                vmem((NX, 2, half_y, piece, sl), BF16),
                vmem((NX, 2, half_y, piece, sl), BF16),
                vmem((NX, piece, sl), F32),
                vmem((2, NZ, 16, hs), BF16),
                vmem((2, NZ, 16, hs), BF16),
                vmem((NT, tokb, sl), BF16),
                vmem((NT, tokb, 128), F32),
                vmem((4 * tokb, NZ * 16), BF16),
                vmem((NX, sl, 2 * hidden), BF16),
                vmem((NX, hidden, sl), BF16),
                vmem((rows, hidden), BF16),
                vmem((rows, 2 * hidden), BF16),
                vmem((NX, sl, hidden), BF16),
                vmem((NX, sl, hidden), BF16),
                vmem((NX, hidden, sl), BF16),
                dma((3 * NX,)),
                dma((NZ,)), dma((NZ,)), dma((NZ,)), dma((NZ,)),
                dma((2, NY, 2)), dma((NX, 2, half_y)),
                dma(()), dma(()), dma(()),
                dma((NX,)), dma((NX,)),
                dma((2, 3)), dma((2, 3)),
                dma((NX, 2, half_y)), dma((NX, 2, half_y)),
                dma((2, NT)), dma((2, NT)),
                dma((3 * NX,)),
            ],
            compiler_params=pltpu.CompilerParams(
                collective_id=0, has_side_effects=True, vmem_limit_bytes=56 * 2**20
            ),
        )(expert_ids, combine, tokens, grad_out, gate_weight, up_weight, down_weight)

    return jax.shard_map(
        step,
        mesh=mesh,
        in_specs=(
            P("ep", None),
            P("ep", None),
            P("ep", None),
            P("ep", None),
            P(None, ("ep", "tp")),
            P(None, ("ep", "tp")),
            P(("ep", "tp"), None),
        ),
        out_specs=(
            P("ep", None),
            P("ep", None),
            P("ep", None),
            P(None, ("ep", "tp")),
            P(None, ("ep", "tp")),
            P(("ep", "tp"), None),
        ),
        check_vma=False,
    )
```

```python
import functools

import jax
import jax.numpy as jnp
from jax import lax
from jax.experimental import pallas as pl
from jax.experimental.pallas import tpu as pltpu
from jax.sharding import PartitionSpec as P

CAP = 6
CORES = 2
MESH = pl.DeviceIdType.MESH
F32 = jnp.float32
BF16 = jnp.bfloat16


def dot_nn(a, b):
    return jnp.dot(a, b, preferred_element_type=F32)


def dot_nt(a, b):
    return lax.dot_general(a, b, (((1,), (1,)), ((), ())), preferred_element_type=F32)


def dot_tn(a, b):
    return lax.dot_general(a, b, (((0,), (0,)), ((), ())), preferred_element_type=F32)


def kernel(
    dims,
    ids_ref, comb_ref, tok_hbm, go_hbm, gate_hbm, up_hbm, down_hbm,
    mixed_ref, gtok_ref, gcomb_ref, gg_ref, gu_ref, gd_ref,
    xg, part, xs, xr, ys, yr, res,
    slab_out, slab_in, fin, fsc, pick, src, gos, wgu, wd, hid, dgu,
    w_sem, t_sem, za_s, za_r, zb_s, zb_r, gx, gy, g_send, d_send, d_recv,
    p_send, p_recv, rx_s, rx_r, ry_s, ry_r, f_s, f_r,
):
    NX, NY, NZ, CAPA = dims
    PIECE = NZ * CAPA
    TOKB, D = tok_hbm.shape
    SL = D // NX
    HS = SL // 2
    ROWS = NY * PIECE
    PER = NX * NY
    HID = wd.shape[1] // 2

    ep, tp = lax.axis_index("ep"), lax.axis_index("tp")
    c, x = lax.rem(tp, CORES), lax.div(tp, CORES)
    y, z = lax.rem(ep, NY), lax.div(ep, NY)

    def wx(v):
        return lax.rem(v + 2 * NX, NX)

    def wy(v):
        return lax.rem(v + 2 * NY, NY)

    def at(xx, yy, zz, cc):
        return (zz * NY + yy, xx * CORES + cc)

    yup, ydown = at(x, wy(y + 1), z, c), at(x, wy(y - 1), z, c)
    sibling = at(x, y, z, 1 - c)

    def remote(src, dst, ssem, rsem, device):
        return pltpu.make_async_remote_copy(
            src_ref=src, dst_ref=dst, send_sem=ssem, recv_sem=rsem,
            device_id=device, device_id_type=MESH,
        )

    def arrived(dst, rsem):
        remote(dst, dst, rsem, rsem, sibling).wait_recv()

    def sent(src, ssem):
        remote(src, src, ssem, ssem, sibling).wait_send()

    barrier = pltpu.get_barrier_semaphore()
    peers_z = [at(x, y, lax.rem(z + d, NZ), c) for d in range(1, NZ)]
    NT = NX * CORES
    peers_t = [(ep, lax.rem(tp + d, NT)) for d in range(1, NT)]
    far_up, far_down = at(x, wy(y + 2), z, c), at(x, wy(y - 2), z, c)
    partners = peers_z + peers_t + [yup, ydown, far_up, far_down]
    ynear, yfar = (yup, ydown), (far_up, far_down)
    xdev = [at(wx(x + k), y, z, c) for k in (2, 1, NX - 1)]
    for device in partners:
        pl.semaphore_signal(barrier, inc=1, device_id=device, device_id_type=MESH)

    features = pl.ds(pl.multiple_of(x * SL, 128), SL)

    @pl.when(c == 0)
    def _():
        pltpu.make_async_copy(tok_hbm.at[:, features], src, t_sem.at[0]).start()

    @pl.when(c == 1)
    def _():
        pltpu.make_async_copy(go_hbm.at[:, features], src, t_sem.at[0]).start()

    load_go = pltpu.make_async_copy(go_hbm.at[:, features], gos, t_sem.at[1])
    load_go.start()
    own_units, sib_units = (pl.ds(0, HID), pl.ds(HID, HID))
    own_pair, sib_pair = (pl.ds(0, 2 * HID), pl.ds(2 * HID, 2 * HID))
    loads = []
    for i in range(NX):
        rows = pl.ds(i * SL, SL)
        loads.append(pltpu.make_async_copy(gate_hbm.at[rows, :], wgu.at[i, :, pl.ds(0, HID)], w_sem.at[3 * i]))
        loads.append(pltpu.make_async_copy(up_hbm.at[rows, :], wgu.at[i, :, pl.ds(HID, HID)], w_sem.at[3 * i + 1]))
        loads.append(pltpu.make_async_copy(down_hbm.at[:, rows], wd.at[i, own_units], w_sem.at[3 * i + 2]))
    for load in loads:
        load.start()

    lane = lax.broadcasted_iota(jnp.int32, (TOKB, NZ * 16), 1)
    expert, place = lax.shift_right_logical(lane, 4), lane & 15
    diagonal = lax.broadcasted_iota(jnp.int32, (TOKB, TOKB), 0) == lax.broadcasted_iota(jnp.int32, (TOKB, TOKB), 1)

    def column(ref, k):
        return jnp.sum(jnp.where(diagonal, ref[k : k + 1, :].astype(F32), 0.0), axis=1, keepdims=True)

    id0, id1 = column(ids_ref, 0).astype(jnp.int32), column(ids_ref, 1).astype(jnp.int32)
    cw0, cw1 = column(comb_ref, 0), column(comb_ref, 1)
    is0, is1 = id0 == expert, id1 == expert
    named = jnp.where(is0 | is1, 1.0, 0.0)
    earlier = jnp.where(
        lax.broadcasted_iota(jnp.int32, (TOKB, TOKB), 0) > lax.broadcasted_iota(jnp.int32, (TOKB, TOKB), 1), 1.0, 0.0
    )
    rank = dot_nn(earlier.astype(BF16), named.astype(BF16)).astype(jnp.int32)
    hit0 = rank == place
    hit1 = (rank + CAPA == place) & (rank < CAPA)
    hit0 = hit0 & (place < CAPA)
    for g, mask in enumerate((is0 & hit0, is1 & hit0, is0 & hit1, is1 & hit1)):
        pick[g * TOKB : (g + 1) * TOKB, :] = jnp.where(mask, 1.0, 0.0).astype(BF16)

    one = jnp.ones((TOKB, 1), F32)
    w0 = jnp.where(c == 0, one, cw0)
    w1 = jnp.where(c == 0, one, cw1)
    spans = (slice(0, HS), slice(HS, SL))
    pltpu.make_async_copy(gos, src, t_sem.at[0]).wait()
    sources = []
    for span in spans:
        v = src[:, span].astype(F32)
        sources += [(v * w0).astype(BF16), (v * w1).astype(BF16)]
    slabs = dot_tn(pick[...], jnp.concatenate(sources, axis=0)).astype(BF16)
    for e in range(NZ):
        slab_out[0, e] = slabs[e * 16 : (e + 1) * 16]
    slab_in[0, z] = slab_out[0, z]

    pl.semaphore_wait(barrier, len(partners))

    def give_weights():
        for load in loads:
            load.wait()

        @pl.when(c == 0)
        def _():
            remote(wgu.at[:, :, own_pair], wgu.at[:, :, sib_pair], p_send.at[0], p_recv.at[0], sibling).start()

        @pl.when(c == 1)
        def _():
            remote(wd.at[:, own_units], wd.at[:, sib_units], p_send.at[0], p_recv.at[0], sibling).start()

    def exchange_z(which, s_sem, r_sem):
        for d in range(1, NZ):
            remote(
                slab_out.at[which, lax.rem(z + d, NZ)], slab_in.at[which, z],
                s_sem.at[d], r_sem.at[d], peers_z[d - 1],
            ).start()
        if which == 0:
            give_weights()
        for d in range(1, NZ):
            arrived(slab_in.at[which, lax.rem(z - d + NZ, NZ)], r_sem.at[d])

    exchange_z(0, za_s, za_r)

    row = lax.broadcasted_iota(jnp.int32, (PIECE, NZ * 16), 0)
    col = lax.broadcasted_iota(jnp.int32, (PIECE, NZ * 16), 1)
    block, inner = lax.shift_right_logical(col, 4), col & 15
    tidy0 = jnp.where((block * CAPA + inner == row) & (inner < CAPA), 1.0, 0.0).astype(BF16)
    tidy1 = jnp.where(
        (block * CAPA + inner - CAPA == row) & (inner >= CAPA) & (inner < 2 * CAPA), 1.0, 0.0
    ).astype(BF16)
    got = slab_in[0].reshape(NZ * 16, HS)
    mine = c * PER + x * NY + y
    xg[mine, :, 0:HS] = dot_nn(tidy0, got).astype(BF16)
    xg[mine, :, HS:SL] = dot_nn(tidy1, got).astype(BF16)

    halves = (pl.ds(0, HS), pl.ds(HS, HS))
    HY = NY // 2
    order = (0, -1, 1, -2, 2, -3, 3, HY)

    def to_sibling(p):
        remote(xg.at[p], xg.at[p], d_send, d_recv, sibling).start()

    def send(ref, sem, device):
        remote(ref, ref, g_send, sem, device).start()

    def along_x(p, i):
        for k in range(NX - 1):
            send(xg.at[p], gx.at[k, i], xdev[k])

    def from_x(k):
        return wx(x - (2, 1, -1)[k])

    def begin_y(j, p, short):
        for d in range(2):
            if short:
                send(xg.at[p], gy.at[j, d, 1], yfar[d])
            send(xg.at[p], gy.at[j, d, 0], ynear[d])

    def onward_y(j, d, s, piece_at, short):
        p = piece_at(wy(y - s - 1 if d == 0 else y + s + 1))
        if s == HY - 1:
            arrived(xg.at[p, :, halves[d]], gy.at[j, d, s])
            return p
        arrived(xg.at[p], gy.at[j, d, s])
        if s == 0 and not short:
            send(xg.at[p], gy.at[j, d, 1], ynear[d])
        if s == 1:
            send(xg.at[p], gy.at[j, d, 2], ynear[d])
            send(xg.at[p, :, halves[d]], gy.at[j, d, 3], yfar[d])
        return p

    def gather_y_then_x():
        def piece_at(yy):
            return x * NY + yy

        p = piece_at(y)
        begin_y(0, p, True)
        along_x(p, 0)
        to_sibling(p)
        for s in range(HY):
            for d in range(2):
                p = onward_y(0, d, s, piece_at, True)
                if s < HY - 1 or d == 1:
                    along_x(p, 2 * s + 1 if s == HY - 1 else 2 * s + 1 + d)
                    to_sibling(p)
        for i in range(NY):
            for k in range(NX - 1):
                p = from_x(k) * NY + wy(y + order[i])
                arrived(xg.at[p], gx.at[k, i])
                to_sibling(p)

    def gather_x_then_y():
        def piece_of(xx):
            return lambda yy: PER + xx * NY + yy

        p = piece_of(x)(y)
        along_x(p, 0)
        begin_y(0, p, False)
        to_sibling(p)
        streams = [(0, piece_of(x))] + [(1 + k, piece_of(from_x(k))) for k in (1, 2, 0)]
        for j, piece_at in streams[1:]:
            p = piece_at(y)
            arrived(xg.at[p], gx.at[j - 1, 0])
            begin_y(j, p, False)
            to_sibling(p)
        for s in range(HY):
            for j, piece_at in streams:
                for d in range(2):
                    p = onward_y(j, d, s, piece_at, False)
                    if s < HY - 1 or d == 1:
                        to_sibling(p)

    pl.when(c == 0)(gather_y_then_x)
    pl.when(c == 1)(gather_x_then_y)
    arrived(xg.at[pl.ds((1 - c) * PER, PER)], d_recv)

    def rows_of(a, i):
        return xg[a * PER + i * NY : a * PER + (i + 1) * NY].reshape(ROWS, SL)

    pre = dot_nn(rows_of(0, 0), wgu[0, :, own_pair])
    d_hidden = dot_nt(rows_of(1, 0), wd[0, own_units])
    for i in range(1, NX):
        pre = pre + dot_nn(rows_of(0, i), wgu[i, :, own_pair])
        d_hidden = d_hidden + dot_nt(rows_of(1, i), wd[i, own_units])
    gate_pre, up_pre = pre[:, :HID], pre[:, HID:]
    sigma = jax.nn.sigmoid(gate_pre)
    silu = gate_pre * sigma
    hid[:, own_units] = (silu * up_pre).astype(BF16)
    dgu[:, pl.ds(0, HID)] = (d_hidden * up_pre * sigma * (1.0 + gate_pre * (1.0 - sigma))).astype(BF16)
    dgu[:, pl.ds(HID, HID)] = (d_hidden * silu).astype(BF16)

    @pl.when(c == 0)
    def _():
        remote(dgu.at[:, own_pair], dgu.at[:, sib_pair], p_send.at[1], p_recv.at[1], sibling).start()

    @pl.when(c == 1)
    def _():
        remote(hid.at[:, own_units], hid.at[:, sib_units], p_send.at[1], p_recv.at[1], sibling).start()

    def weight_grads(first, last):
        def step(i, carry):
            rows_x = xg[pl.ds(i * NY, NY)].reshape(ROWS, SL)
            rows_g = xg[pl.ds(PER + i * NY, NY)].reshape(ROWS, SL)
            both = dot_tn(rows_x, dgu[:, own_pair])
            span = pl.ds(pl.multiple_of(i * SL, 128), SL)
            gg_ref[span, :] = both[:, :HID].astype(BF16)
            gu_ref[span, :] = both[:, HID:].astype(BF16)
            gd_ref[:, span] = dot_tn(hid[:, own_units], rows_g).astype(BF16)
            return carry

        lax.fori_loop(first, last, step, 0)

    weight_grads(0, NX // 2)

    def partial_chunk(j, carry):
        xx = wx(x + 2 - j)
        span = pl.ds(xx * NY, NY)

        @pl.when(c == 0)
        def _():
            part[span] = dot_nn(hid[...], wd[xx]).reshape(NY, PIECE, SL)

        @pl.when(c == 1)
        def _():
            part[span] = dot_nt(dgu[...], wgu[xx]).reshape(NY, PIECE, SL)

        return carry

    @pl.when(c == 0)
    def _():
        arrived(wd.at[:, sib_units], p_recv.at[0])
        arrived(hid.at[:, sib_units], p_recv.at[1])

    @pl.when(c == 1)
    def _():
        arrived(wgu.at[:, :, sib_pair], p_recv.at[0])
        arrived(dgu.at[:, sib_pair], p_recv.at[1])

    lax.fori_loop(0, NX, partial_chunk, 0)

    def own(p):
        return part[p]

    def y_out(j, d, s, v):
        out, into = ys.at[j, d, s], yr.at[j, d, s]
        if s == HY - 1:
            out, into = out.at[:, halves[d]], into.at[:, halves[d]]
            v = v[:, :HS] if d == 0 else v[:, HS:]
        out[...] = v.astype(BF16)
        hop = yfar if s == HY - 1 or (s == 1 and c_short[0]) else ynear
        remote(out, into, ry_s.at[j, d, s], ry_r.at[j, d, s], hop[d]).start()

    def y_came(j, d, s):
        into = yr.at[j, d, s]
        if s == HY - 1:
            into = into.at[:, halves[d]]
        arrived(into, ry_r.at[j, d, s])
        return into[...].astype(F32)

    def y_first(j, get):
        for d in range(2):
            y_out(j, d, 2, get(3 - 6 * d))
        v = get(HY)
        for d in range(2):
            y_out(j, d, 3, v)

    def y_second(j, d, get):
        v = get(2 - 4 * d) + y_came(j, d, 2)
        half = y_came(j, d, 3)
        lo, hi = v[:, :HS], v[:, HS:]
        lo, hi = (lo + half, hi) if d == 0 else (lo, hi + half)
        y_out(j, d, 1, jnp.concatenate([lo, hi], axis=1))

    def x_out(k, i, v):
        xs[k, i] = v.astype(BF16)
        remote(xs.at[k, i], xr.at[k, i], rx_s.at[k, i], rx_r.at[k, i], xdev[k]).start()

    def x_came(i):
        v = None
        for k in range(NX - 1):
            arrived(xr.at[k, i], rx_r.at[k, i])
            w = xr[k, i].astype(F32)
            v = w if v is None else v + w
        return v

    c_short = [False]
    back_order = (3, -3, HY, 2, -2, 1, -1, 0)
    chunk_of = (0, 1, 3)

    def at_y(off):
        return wy(y + off)

    def begin_x_then_y():
        for i, off in enumerate(back_order):
            for k in range(NX - 1):
                x_out(k, i, own(wx(x + 2 - chunk_of[k]) * NY + at_y(off)))

    def begin_y_then_x():
        for j in range(NX):
            y_first(j, lambda off: own(wx(x + 2 - j) * NY + at_y(off)))

    pl.when(c == 0)(begin_x_then_y)
    pl.when(c == 1)(begin_y_then_x)

    weight_grads(NX // 2, NX)

    def end_x_then_y():
        c_short[0] = True

        def get(off):
            return own(x * NY + at_y(off)) + x_came(back_order.index(off))

        y_first(0, get)
        for d in range(2):
            y_second(0, d, get)
        for d in range(2):
            y_out(0, d, 0, get(1 - 2 * d))
        v = get(0)
        for s in range(2):
            for d in range(2):
                v = v + y_came(0, d, s)
        res[x] = v

    def end_y_then_x():
        c_short[0] = False

        def get(j):
            return lambda off: own(wx(x + 2 - j) * NY + at_y(off))

        for j in range(NX):
            for d in range(2):
                y_second(j, d, get(j))
        for j in range(NX):
            for d in range(2):
                y_out(j, d, 0, get(j)(1 - 2 * d) + y_came(j, d, 1))
        for j in range(NX):
            v = get(j)(0) + y_came(j, 0, 0) + y_came(j, 1, 0)
            if j in chunk_of:
                x_out(chunk_of.index(j), 0, v)
            else:
                res[x] = v
        res[x] = res[x] + x_came(0)

    pl.when(c == 0)(end_x_then_y)
    pl.when(c == 1)(end_y_then_x)

    done = res[x].astype(BF16)
    back = (dot_tn(tidy0, done[:, :HS]) + dot_tn(tidy1, done[:, HS:])).astype(BF16)
    for e in range(NZ):
        slab_out[1, e] = back[e * 16 : (e + 1) * 16]
    slab_in[1, z] = slab_out[1, z]
    exchange_z(1, zb_s, zb_r)
    chosen = dot_nn(pick[...], slab_in[1].reshape(NZ * 16, HS))
    c0 = jnp.where(c == 0, cw0, one)
    c1 = jnp.where(c == 0, cw1, one)
    scores = [jnp.zeros((TOKB, 1), F32), jnp.zeros((TOKB, 1), F32)]
    load_go.wait()
    for h, span in enumerate(spans):
        first = chosen[2 * h * TOKB : (2 * h + 1) * TOKB]
        second = chosen[(2 * h + 1) * TOKB : (2 * h + 2) * TOKB]
        fin[tp, :, h * HS : (h + 1) * HS] = (c0 * first + c1 * second).astype(BF16)
        g = gos[:, span].astype(F32)
        scores[0] = scores[0] + jnp.sum(g * first, axis=1, keepdims=True)
        scores[1] = scores[1] + jnp.sum(g * second, axis=1, keepdims=True)
    lane = lax.broadcasted_iota(jnp.int32, (TOKB, 128), 1)
    fsc[tp] = jnp.where(lane == 0, scores[0], jnp.where(lane == 1, scores[1], 0.0))

    for d in range(1, NT):
        remote(fin.at[tp], fin.at[tp], f_s.at[0, d], f_r.at[0, d], peers_t[d - 1]).start()
        remote(fsc.at[tp], fsc.at[tp], f_s.at[1, d], f_r.at[1, d], peers_t[d - 1]).start()
    for d in range(1, NT):
        source = lax.rem(tp - d + NT, NT)
        arrived(fin.at[source], f_r.at[0, d])
        arrived(fsc.at[source], f_r.at[1, d])
    total_score = fsc[0]
    for i in range(NX):
        mixed_ref[:, i * SL : (i + 1) * SL] = fin[CORES * i]
        gtok_ref[:, i * SL : (i + 1) * SL] = fin[CORES * i + 1]
        if i:
            total_score = total_score + fsc[CORES * i]
    for k in range(2):
        gcomb_ref[k : k + 1, :] = jnp.sum(jnp.where(diagonal, total_score[:, k : k + 1], 0.0), axis=0, keepdims=True)

    for d in range(1, NZ):
        sent(slab_out.at[0, 0], za_s.at[d])
        sent(slab_out.at[1, 0], zb_s.at[d])
    for d in range(1, NT):
        sent(fin.at[tp], f_s.at[0, d])
        sent(fsc.at[tp], f_s.at[1, d])
    sent(xg.at[pl.ds(0, PER - 1)], g_send)
    sent(xg.at[pl.ds(c * PER, PER)], d_send)

    def y_sent(j):
        for d in range(2):
            sent(ys.at[j, d, HY - 1].at[:, halves[d]], ry_s.at[j, d, HY - 1])
            for t in range(HY - 1):
                sent(ys.at[j, d, t], ry_s.at[j, d, t])

    @pl.when(c == 0)
    def _():
        sent(wgu.at[:, :, own_pair], p_send.at[0])
        sent(dgu.at[:, own_pair], p_send.at[1])
        for k in range(NX - 1):
            for i in range(NY):
                sent(xs.at[k, i], rx_s.at[k, i])
        y_sent(0)

    @pl.when(c == 1)
    def _():
        sent(wd.at[:, own_units], p_send.at[0])
        sent(hid.at[:, own_units], p_send.at[1])
        for k in range(NX - 1):
            sent(xs.at[k, 0], rx_s.at[k, 0])
        for j in range(NX):
            y_sent(j)


def solution(mesh, cap=CAP, planes=8):
    NT = mesh.shape["tp"]
    NX, NZ = NT // CORES, planes
    NY = mesh.shape["ep"] // NZ

    def step(tokens, expert_ids, combine, grad_out, gate_weight, up_weight, down_weight):
        tokb, d = tokens.shape
        hidden = gate_weight.shape[1]
        sl, piece, per = d // NX, NZ * cap, NX * NY
        hs, rows, half_y = sl // 2, NY * piece, NY // 2
        dma, vmem, hbm = pltpu.SemaphoreType.DMA, pltpu.VMEM, pl.BlockSpec(memory_space=pl.ANY)
        held = pl.BlockSpec(memory_space=pltpu.VMEM)
        mixed, gtok, gcomb, gg, gu, gd = pl.pallas_call(
            functools.partial(kernel, (NX, NY, NZ, cap)),
            out_shape=(
                vmem((tokb, d), BF16),
                vmem((tokb, d), BF16),
                vmem(combine.shape[::-1], F32),
                vmem(gate_weight.shape, BF16),
                vmem(up_weight.shape, BF16),
                vmem(down_weight.shape, BF16),
            ),
            in_specs=[held] * 2 + [hbm] * 5,
            out_specs=[held] * 6,
            scratch_shapes=[
                vmem((2 * per, piece, sl), BF16),
                vmem((per, piece, sl), F32),
                vmem((NX - 1, NY, piece, sl), BF16),
                vmem((NX - 1, NY, piece, sl), BF16),
                vmem((NX, 2, half_y, piece, sl), BF16),
                vmem((NX, 2, half_y, piece, sl), BF16),
                vmem((NX, piece, sl), F32),
                vmem((2, NZ, 16, hs), BF16),
                vmem((2, NZ, 16, hs), BF16),
                vmem((NT, tokb, sl), BF16),
                vmem((NT, tokb, 128), F32),
                vmem((4 * tokb, NZ * 16), BF16),
                vmem((tokb, sl), BF16), vmem((tokb, sl), BF16),
                vmem((NX, sl, 4 * hidden), BF16),
                vmem((NX, 2 * hidden, sl), BF16),
                vmem((rows, 2 * hidden), BF16),
                vmem((rows, 4 * hidden), BF16),
                dma((3 * NX,)), dma((2,)),
                dma((NZ,)), dma((NZ,)), dma((NZ,)), dma((NZ,)),
                dma((NX - 1, NY)), dma((NX, 2, half_y)),
                dma(()), dma(()), dma(()),
                dma((2,)), dma((2,)),
                dma((NX - 1, NY)), dma((NX - 1, NY)),
                dma((NX, 2, half_y)), dma((NX, 2, half_y)),
                dma((2, NT)), dma((2, NT)),
            ],
            compiler_params=pltpu.CompilerParams(
                collective_id=0, has_side_effects=True, vmem_limit_bytes=56 * 2**20
            ),
        )(expert_ids.T, combine.T, tokens, grad_out, gate_weight, up_weight, down_weight)
        return mixed, gtok, gcomb.T, gg, gu, gd

    return jax.shard_map(
        step,
        mesh=mesh,
        in_specs=(
            P("ep", None),
            P("ep", None),
            P("ep", None),
            P("ep", None),
            P(None, ("ep", "tp")),
            P(None, ("ep", "tp")),
            P(("ep", "tp"), None),
        ),
        out_specs=(
            P("ep", None),
            P("ep", None),
            P("ep", None),
            P(None, ("ep", "tp")),
            P(None, ("ep", "tp")),
            P(("ep", "tp"), None),
        ),
        check_vma=False,
    )
```

```python
import functools

import jax
import jax.numpy as jnp
from jax import lax
from jax.experimental import pallas as pl
from jax.experimental.pallas import tpu as pltpu
from jax.sharding import PartitionSpec as P

CAP = 6
CORES = 2
MESH = pl.DeviceIdType.MESH
F32 = jnp.float32
BF16 = jnp.bfloat16


def dot_nn(a, b):
    return jnp.dot(a, b, preferred_element_type=F32)


def dot_nt(a, b):
    return lax.dot_general(a, b, (((1,), (1,)), ((), ())), preferred_element_type=F32)


def dot_tn(a, b):
    return lax.dot_general(a, b, (((0,), (0,)), ((), ())), preferred_element_type=F32)


def kernel(
    dims,
    ids_ref, comb_ref, tok_hbm, go_hbm, gate_hbm, up_hbm, down_hbm,
    mixed_ref, gtok_ref, gcomb_ref, gg_ref, gu_ref, gd_ref,
    xg, part, xs, xr, ys, yr, res,
    slab_out, slab_in, fin, fsc, pick, src, gos, wgu, wd, hid, dgu,
    w_sem, t_sem, za_s, za_r, zb_s, zb_r, gx, gy, g_send, d_send, d_recv,
    p_send, p_recv, rx_s, rx_r, ry_s, ry_r, f_s, f_r,
):
    NX, NY, NZ, CAPA = dims
    PIECE = NZ * CAPA
    TOKB, D = tok_hbm.shape
    SL = D // NX
    HS = SL // 2
    ROWS = NY * PIECE
    PER = NX * NY
    HID = wd.shape[1] // 2

    ep, tp = lax.axis_index("ep"), lax.axis_index("tp")
    c, x = lax.rem(tp, CORES), lax.div(tp, CORES)
    y, z = lax.rem(ep, NY), lax.div(ep, NY)

    def wx(v):
        return lax.rem(v + 2 * NX, NX)

    def wy(v):
        return lax.rem(v + 2 * NY, NY)

    def at(xx, yy, zz, cc):
        return (zz * NY + yy, xx * CORES + cc)

    yup, ydown = at(x, wy(y + 1), z, c), at(x, wy(y - 1), z, c)
    sibling = at(x, y, z, 1 - c)

    def remote(src, dst, ssem, rsem, device):
        return pltpu.make_async_remote_copy(
            src_ref=src, dst_ref=dst, send_sem=ssem, recv_sem=rsem,
            device_id=device, device_id_type=MESH,
        )

    def arrived(dst, rsem):
        remote(dst, dst, rsem, rsem, sibling).wait_recv()

    def sent(src, ssem):
        remote(src, src, ssem, ssem, sibling).wait_send()

    barrier = pltpu.get_barrier_semaphore()
    peers_z = [at(x, y, lax.rem(z + d, NZ), c) for d in range(1, NZ)]
    NT = NX * CORES
    peers_t = [(ep, lax.rem(tp + d, NT)) for d in range(1, NT)]
    far_up, far_down = at(x, wy(y + 2), z, c), at(x, wy(y - 2), z, c)
    partners = peers_z + peers_t + [yup, ydown, far_up, far_down]
    ynear, yfar = (yup, ydown), (far_up, far_down)
    xdev = [at(wx(x + k), y, z, c) for k in (2, 1, NX - 1)]
    for device in partners:
        pl.semaphore_signal(barrier, inc=1, device_id=device, device_id_type=MESH)

    features = pl.ds(pl.multiple_of(x * SL, 128), SL)

    @pl.when(c == 0)
    def _():
        pltpu.make_async_copy(tok_hbm.at[:, features], src, t_sem.at[0]).start()

    @pl.when(c == 1)
    def _():
        pltpu.make_async_copy(go_hbm.at[:, features], src, t_sem.at[0]).start()

    load_go = pltpu.make_async_copy(go_hbm.at[:, features], gos, t_sem.at[1])
    load_go.start()
    own_units, sib_units = (pl.ds(0, HID), pl.ds(HID, HID))
    own_pair, sib_pair = (pl.ds(0, 2 * HID), pl.ds(2 * HID, 2 * HID))
    loads = []
    for i in range(NX):
        rows = pl.ds(i * SL, SL)
        loads.append(pltpu.make_async_copy(gate_hbm.at[rows, :], wgu.at[i, :, pl.ds(0, HID)], w_sem.at[3 * i]))
        loads.append(pltpu.make_async_copy(up_hbm.at[rows, :], wgu.at[i, :, pl.ds(HID, HID)], w_sem.at[3 * i + 1]))
        loads.append(pltpu.make_async_copy(down_hbm.at[:, rows], wd.at[i, own_units], w_sem.at[3 * i + 2]))
    for load in loads:
        load.start()

    lane = lax.broadcasted_iota(jnp.int32, (TOKB, NZ * 16), 1)
    expert, place = lax.shift_right_logical(lane, 4), lane & 15
    diagonal = lax.broadcasted_iota(jnp.int32, (TOKB, TOKB), 0) == lax.broadcasted_iota(jnp.int32, (TOKB, TOKB), 1)

    def column(ref, k):
        return jnp.sum(jnp.where(diagonal, ref[k : k + 1, :].astype(F32), 0.0), axis=1, keepdims=True)

    id0, id1 = column(ids_ref, 0).astype(jnp.int32), column(ids_ref, 1).astype(jnp.int32)
    cw0, cw1 = column(comb_ref, 0), column(comb_ref, 1)
    is0, is1 = id0 == expert, id1 == expert
    named = jnp.where(is0 | is1, 1.0, 0.0)
    earlier = jnp.where(
        lax.broadcasted_iota(jnp.int32, (TOKB, TOKB), 0) > lax.broadcasted_iota(jnp.int32, (TOKB, TOKB), 1), 1.0, 0.0
    )
    rank = dot_nn(earlier.astype(BF16), named.astype(BF16)).astype(jnp.int32)
    hit0 = rank == place
    hit1 = (rank + CAPA == place) & (rank < CAPA)
    hit0 = hit0 & (place < CAPA)
    for g, mask in enumerate((is0 & hit0, is1 & hit0, is0 & hit1, is1 & hit1)):
        pick[g * TOKB : (g + 1) * TOKB, :] = jnp.where(mask, 1.0, 0.0).astype(BF16)

    one = jnp.ones((TOKB, 1), F32)
    w0 = jnp.where(c == 0, one, cw0)
    w1 = jnp.where(c == 0, one, cw1)
    spans = (slice(0, HS), slice(HS, SL))
    pltpu.make_async_copy(gos, src, t_sem.at[0]).wait()
    sources = []
    for span in spans:
        v = src[:, span].astype(F32)
        sources += [(v * w0).astype(BF16), (v * w1).astype(BF16)]
    slabs = dot_tn(pick[...], jnp.concatenate(sources, axis=0)).astype(BF16)
    for e in range(NZ):
        slab_out[0, e] = slabs[e * 16 : (e + 1) * 16]
    slab_in[0, z] = slab_out[0, z]

    pl.semaphore_wait(barrier, len(partners))

    def give_weights():
        for load in loads:
            load.wait()

        @pl.when(c == 0)
        def _():
            remote(wgu.at[:, :, own_pair], wgu.at[:, :, sib_pair], p_send.at[0], p_recv.at[0], sibling).start()

        @pl.when(c == 1)
        def _():
            remote(wd.at[:, own_units], wd.at[:, sib_units], p_send.at[0], p_recv.at[0], sibling).start()

    def exchange_z(which, s_sem, r_sem):
        for d in range(1, NZ):
            remote(
                slab_out.at[which, lax.rem(z + d, NZ)], slab_in.at[which, z],
                s_sem.at[d], r_sem.at[d], peers_z[d - 1],
            ).start()
        if which == 0:
            give_weights()
        for d in range(1, NZ):
            arrived(slab_in.at[which, lax.rem(z - d + NZ, NZ)], r_sem.at[d])

    exchange_z(0, za_s, za_r)

    row = lax.broadcasted_iota(jnp.int32, (PIECE, NZ * 16), 0)
    col = lax.broadcasted_iota(jnp.int32, (PIECE, NZ * 16), 1)
    block, inner = lax.shift_right_logical(col, 4), col & 15
    tidy0 = jnp.where((block * CAPA + inner == row) & (inner < CAPA), 1.0, 0.0).astype(BF16)
    tidy1 = jnp.where(
        (block * CAPA + inner - CAPA == row) & (inner >= CAPA) & (inner < 2 * CAPA), 1.0, 0.0
    ).astype(BF16)
    got = slab_in[0].reshape(NZ * 16, HS)
    mine = c * PER + x * NY + y
    xg[mine, :, 0:HS] = dot_nn(tidy0, got).astype(BF16)
    xg[mine, :, HS:SL] = dot_nn(tidy1, got).astype(BF16)

    halves = (pl.ds(0, HS), pl.ds(HS, HS))
    HY = NY // 2
    order = (0, -1, 1, -2, 2, -3, 3, HY)

    def to_sibling(p):
        remote(xg.at[p], xg.at[p], d_send, d_recv, sibling).start()

    def send(ref, sem, device):
        remote(ref, ref, g_send, sem, device).start()

    def along_x(p, i):
        for k in range(NX - 1):
            send(xg.at[p], gx.at[k, i], xdev[k])

    def from_x(k):
        return wx(x - (2, 1, -1)[k])

    def begin_y(j, p, short):
        for d in range(2):
            if short:
                send(xg.at[p], gy.at[j, d, 1], yfar[d])
            send(xg.at[p], gy.at[j, d, 0], ynear[d])

    def onward_y(j, d, s, piece_at, short):
        p = piece_at(wy(y - s - 1 if d == 0 else y + s + 1))
        if s == HY - 1:
            arrived(xg.at[p, :, halves[d]], gy.at[j, d, s])
            return p
        arrived(xg.at[p], gy.at[j, d, s])
        if s == 0 and not short:
            send(xg.at[p], gy.at[j, d, 1], ynear[d])
        if s == 1:
            send(xg.at[p], gy.at[j, d, 2], ynear[d])
            send(xg.at[p, :, halves[d]], gy.at[j, d, 3], yfar[d])
        return p

    def gather_y_then_x():
        def piece_at(yy):
            return x * NY + yy

        p = piece_at(y)
        begin_y(0, p, True)
        along_x(p, 0)
        to_sibling(p)
        for s in range(HY):
            for d in range(2):
                p = onward_y(0, d, s, piece_at, True)
                if s < HY - 1 or d == 1:
                    along_x(p, 2 * s + 1 if s == HY - 1 else 2 * s + 1 + d)
                    to_sibling(p)
        for i in range(NY):
            for k in range(NX - 1):
                p = from_x(k) * NY + wy(y + order[i])
                arrived(xg.at[p], gx.at[k, i])
                to_sibling(p)

    def gather_x_then_y():
        def piece_of(xx):
            return lambda yy: PER + xx * NY + yy

        p = piece_of(x)(y)
        along_x(p, 0)
        begin_y(0, p, False)
        to_sibling(p)
        streams = [(0, piece_of(x))] + [(1 + k, piece_of(from_x(k))) for k in (1, 2, 0)]
        for j, piece_at in streams[1:]:
            p = piece_at(y)
            arrived(xg.at[p], gx.at[j - 1, 0])
            begin_y(j, p, False)
            to_sibling(p)
        for s in range(HY):
            for j, piece_at in streams:
                for d in range(2):
                    p = onward_y(j, d, s, piece_at, False)
                    if s < HY - 1 or d == 1:
                        to_sibling(p)

    pl.when(c == 0)(gather_y_then_x)
    pl.when(c == 1)(gather_x_then_y)
    arrived(xg.at[pl.ds((1 - c) * PER, PER)], d_recv)

    def rows_of(a, i):
        return xg[a * PER + i * NY : a * PER + (i + 1) * NY].reshape(ROWS, SL)

    pre = dot_nn(rows_of(0, 0), wgu[0, :, own_pair])
    d_hidden = dot_nt(rows_of(1, 0), wd[0, own_units])
    for i in range(1, NX):
        pre = pre + dot_nn(rows_of(0, i), wgu[i, :, own_pair])
        d_hidden = d_hidden + dot_nt(rows_of(1, i), wd[i, own_units])
    gate_pre, up_pre = pre[:, :HID], pre[:, HID:]
    sigma = jax.nn.sigmoid(gate_pre)
    silu = gate_pre * sigma
    hid[:, own_units] = (silu * up_pre).astype(BF16)
    dgu[:, pl.ds(0, HID)] = (d_hidden * up_pre * sigma * (1.0 + gate_pre * (1.0 - sigma))).astype(BF16)
    dgu[:, pl.ds(HID, HID)] = (d_hidden * silu).astype(BF16)

    @pl.when(c == 0)
    def _():
        remote(dgu.at[:, own_pair], dgu.at[:, sib_pair], p_send.at[1], p_recv.at[1], sibling).start()

    @pl.when(c == 1)
    def _():
        remote(hid.at[:, own_units], hid.at[:, sib_units], p_send.at[1], p_recv.at[1], sibling).start()

    def weight_grads(first, last):
        def step(i, carry):
            rows_x = xg[pl.ds(i * NY, NY)].reshape(ROWS, SL)
            rows_g = xg[pl.ds(PER + i * NY, NY)].reshape(ROWS, SL)
            both = dot_tn(rows_x, dgu[:, own_pair])
            span = pl.ds(pl.multiple_of(i * SL, 128), SL)
            gg_ref[span, :] = both[:, :HID].astype(BF16)
            gu_ref[span, :] = both[:, HID:].astype(BF16)
            gd_ref[:, span] = dot_tn(hid[:, own_units], rows_g).astype(BF16)
            return carry

        lax.fori_loop(first, last, step, 0)

    weight_grads(0, NX // 2)

    def expert_out_chunk(j):
        xx = wx(x + 2 - j)
        part[pl.ds(xx * NY, NY)] = dot_nn(hid[...], wd[xx]).reshape(NY, PIECE, SL)

    def input_grad_chunk(j):
        xx = wx(x + 2 - j)
        part[pl.ds(xx * NY, NY)] = dot_nt(dgu[...], wgu[xx]).reshape(NY, PIECE, SL)

    def own(p):
        return part[p]

    def y_out(j, d, s, v):
        out, into = ys.at[j, d, s], yr.at[j, d, s]
        if s == HY - 1:
            out, into = out.at[:, halves[d]], into.at[:, halves[d]]
            v = v[:, :HS] if d == 0 else v[:, HS:]
        out[...] = v.astype(BF16)
        hop = yfar if s == HY - 1 or (s == 1 and c_short[0]) else ynear
        remote(out, into, ry_s.at[j, d, s], ry_r.at[j, d, s], hop[d]).start()

    def y_came(j, d, s):
        into = yr.at[j, d, s]
        if s == HY - 1:
            into = into.at[:, halves[d]]
        arrived(into, ry_r.at[j, d, s])
        return into[...].astype(F32)

    def y_first(j, get):
        for d in range(2):
            y_out(j, d, 2, get(3 - 6 * d))
        v = get(HY)
        for d in range(2):
            y_out(j, d, 3, v)

    def y_second(j, d, get):
        v = get(2 - 4 * d) + y_came(j, d, 2)
        half = y_came(j, d, 3)
        lo, hi = v[:, :HS], v[:, HS:]
        lo, hi = (lo + half, hi) if d == 0 else (lo, hi + half)
        y_out(j, d, 1, jnp.concatenate([lo, hi], axis=1))

    def x_out(k, i, v):
        xs[k, i] = v.astype(BF16)
        remote(xs.at[k, i], xr.at[k, i], rx_s.at[k, i], rx_r.at[k, i], xdev[k]).start()

    def x_came(i):
        v = None
        for k in range(NX - 1):
            arrived(xr.at[k, i], rx_r.at[k, i])
            w = xr[k, i].astype(F32)
            v = w if v is None else v + w
        return v

    c_short = [False]
    back_order = (3, -3, HY, 2, -2, 1, -1, 0)
    chunk_of = (0, 1, 3)

    def at_y(off):
        return wy(y + off)

    def begin_x_then_y():
        arrived(wd.at[:, sib_units], p_recv.at[0])
        arrived(hid.at[:, sib_units], p_recv.at[1])
        for j in chunk_of:
            expert_out_chunk(j)
        for i, off in enumerate(back_order):
            for k in range(NX - 1):
                x_out(k, i, own(wx(x + 2 - chunk_of[k]) * NY + at_y(off)))
        expert_out_chunk(2)

    def begin_y_then_x():
        arrived(wgu.at[:, :, sib_pair], p_recv.at[0])
        arrived(dgu.at[:, sib_pair], p_recv.at[1])
        for j in range(NX):
            input_grad_chunk(j)
            y_first(j, lambda off: own(wx(x + 2 - j) * NY + at_y(off)))

    pl.when(c == 0)(begin_x_then_y)
    pl.when(c == 1)(begin_y_then_x)

    weight_grads(NX // 2, NX)

    def end_x_then_y():
        c_short[0] = True

        def get(off):
            return own(x * NY + at_y(off)) + x_came(back_order.index(off))

        y_first(0, get)
        for d in range(2):
            y_second(0, d, get)
        for d in range(2):
            y_out(0, d, 0, get(1 - 2 * d))
        v = get(0)
        for s in range(2):
            for d in range(2):
                v = v + y_came(0, d, s)
        res[x] = v

    def end_y_then_x():
        c_short[0] = False

        def get(j):
            return lambda off: own(wx(x + 2 - j) * NY + at_y(off))

        for j in range(NX):
            for d in range(2):
                y_second(j, d, get(j))
        for j in range(NX):
            for d in range(2):
                y_out(j, d, 0, get(j)(1 - 2 * d) + y_came(j, d, 1))
        for j in range(NX):
            v = get(j)(0) + y_came(j, 0, 0) + y_came(j, 1, 0)
            if j in chunk_of:
                x_out(chunk_of.index(j), 0, v)
            else:
                res[x] = v
        res[x] = res[x] + x_came(0)

    pl.when(c == 0)(end_x_then_y)
    pl.when(c == 1)(end_y_then_x)

    done = res[x].astype(BF16)
    back = (dot_tn(tidy0, done[:, :HS]) + dot_tn(tidy1, done[:, HS:])).astype(BF16)
    for e in range(NZ):
        slab_out[1, e] = back[e * 16 : (e + 1) * 16]
    slab_in[1, z] = slab_out[1, z]
    exchange_z(1, zb_s, zb_r)
    chosen = dot_nn(pick[...], slab_in[1].reshape(NZ * 16, HS))
    c0 = jnp.where(c == 0, cw0, one)
    c1 = jnp.where(c == 0, cw1, one)
    scores = [jnp.zeros((TOKB, 1), F32), jnp.zeros((TOKB, 1), F32)]
    load_go.wait()
    for h, span in enumerate(spans):
        first = chosen[2 * h * TOKB : (2 * h + 1) * TOKB]
        second = chosen[(2 * h + 1) * TOKB : (2 * h + 2) * TOKB]
        fin[tp, :, h * HS : (h + 1) * HS] = (c0 * first + c1 * second).astype(BF16)
        g = gos[:, span].astype(F32)
        scores[0] = scores[0] + jnp.sum(g * first, axis=1, keepdims=True)
        scores[1] = scores[1] + jnp.sum(g * second, axis=1, keepdims=True)
    lane = lax.broadcasted_iota(jnp.int32, (TOKB, 128), 1)
    fsc[tp] = jnp.where(lane == 0, scores[0], jnp.where(lane == 1, scores[1], 0.0))

    for d in range(1, NT):
        remote(fin.at[tp], fin.at[tp], f_s.at[0, d], f_r.at[0, d], peers_t[d - 1]).start()
        remote(fsc.at[tp], fsc.at[tp], f_s.at[1, d], f_r.at[1, d], peers_t[d - 1]).start()
    for d in range(1, NT):
        source = lax.rem(tp - d + NT, NT)
        arrived(fin.at[source], f_r.at[0, d])
        arrived(fsc.at[source], f_r.at[1, d])
    total_score = fsc[0]
    for i in range(NX):
        mixed_ref[:, i * SL : (i + 1) * SL] = fin[CORES * i]
        gtok_ref[:, i * SL : (i + 1) * SL] = fin[CORES * i + 1]
        if i:
            total_score = total_score + fsc[CORES * i]
    for k in range(2):
        gcomb_ref[k : k + 1, :] = jnp.sum(jnp.where(diagonal, total_score[:, k : k + 1], 0.0), axis=0, keepdims=True)

    for d in range(1, NZ):
        sent(slab_out.at[0, 0], za_s.at[d])
        sent(slab_out.at[1, 0], zb_s.at[d])
    for d in range(1, NT):
        sent(fin.at[tp], f_s.at[0, d])
        sent(fsc.at[tp], f_s.at[1, d])
    sent(xg.at[pl.ds(0, PER - 1)], g_send)
    sent(xg.at[pl.ds(c * PER, PER)], d_send)

    def y_sent(j):
        for d in range(2):
            sent(ys.at[j, d, HY - 1].at[:, halves[d]], ry_s.at[j, d, HY - 1])
            for t in range(HY - 1):
                sent(ys.at[j, d, t], ry_s.at[j, d, t])

    @pl.when(c == 0)
    def _():
        sent(wgu.at[:, :, own_pair], p_send.at[0])
        sent(dgu.at[:, own_pair], p_send.at[1])
        for k in range(NX - 1):
            for i in range(NY):
                sent(xs.at[k, i], rx_s.at[k, i])
        y_sent(0)

    @pl.when(c == 1)
    def _():
        sent(wd.at[:, own_units], p_send.at[0])
        sent(hid.at[:, own_units], p_send.at[1])
        for k in range(NX - 1):
            sent(xs.at[k, 0], rx_s.at[k, 0])
        for j in range(NX):
            y_sent(j)


def flush(*refs):
    n = len(refs) // 2
    sems = refs[-1]
    copies = [pltpu.make_async_copy(refs[i], refs[n + i], sems.at[i]) for i in range(n)]
    for copy in copies:
        copy.start()
    for copy in copies:
        copy.wait()


def solution(mesh, cap=CAP, planes=8):
    NT = mesh.shape["tp"]
    NX, NZ = NT // CORES, planes
    NY = mesh.shape["ep"] // NZ

    def step(tokens, expert_ids, combine, grad_out, gate_weight, up_weight, down_weight):
        tokb, d = tokens.shape
        hidden = gate_weight.shape[1]
        sl, piece, per = d // NX, NZ * cap, NX * NY
        hs, rows, half_y = sl // 2, NY * piece, NY // 2
        dma, vmem, hbm = pltpu.SemaphoreType.DMA, pltpu.VMEM, pl.BlockSpec(memory_space=pl.ANY)
        held = pl.BlockSpec(memory_space=pltpu.VMEM)
        mixed, gtok, gcomb, gg, gu, gd = pl.pallas_call(
            functools.partial(kernel, (NX, NY, NZ, cap)),
            out_shape=(
                vmem((tokb, d), BF16),
                vmem((tokb, d), BF16),
                vmem(combine.shape[::-1], F32),
                vmem(gate_weight.shape, BF16),
                vmem(up_weight.shape, BF16),
                vmem(down_weight.shape, BF16),
            ),
            in_specs=[held] * 2 + [hbm] * 5,
            out_specs=[held] * 6,
            scratch_shapes=[
                vmem((2 * per, piece, sl), BF16),
                vmem((per, piece, sl), F32),
                vmem((NX - 1, NY, piece, sl), BF16),
                vmem((NX - 1, NY, piece, sl), BF16),
                vmem((NX, 2, half_y, piece, sl), BF16),
                vmem((NX, 2, half_y, piece, sl), BF16),
                vmem((NX, piece, sl), F32),
                vmem((2, NZ, 16, hs), BF16),
                vmem((2, NZ, 16, hs), BF16),
                vmem((NT, tokb, sl), BF16),
                vmem((NT, tokb, 128), F32),
                vmem((4 * tokb, NZ * 16), BF16),
                vmem((tokb, sl), BF16), vmem((tokb, sl), BF16),
                vmem((NX, sl, 4 * hidden), BF16),
                vmem((NX, 2 * hidden, sl), BF16),
                vmem((rows, 2 * hidden), BF16),
                vmem((rows, 4 * hidden), BF16),
                dma((3 * NX,)), dma((2,)),
                dma((NZ,)), dma((NZ,)), dma((NZ,)), dma((NZ,)),
                dma((NX - 1, NY)), dma((NX, 2, half_y)),
                dma(()), dma(()), dma(()),
                dma((2,)), dma((2,)),
                dma((NX - 1, NY)), dma((NX - 1, NY)),
                dma((NX, 2, half_y)), dma((NX, 2, half_y)),
                dma((2, NT)), dma((2, NT)),
            ],
            compiler_params=pltpu.CompilerParams(
                collective_id=0, has_side_effects=True, vmem_limit_bytes=56 * 2**20
            ),
        )(expert_ids.T, combine.T, tokens, grad_out, gate_weight, up_weight, down_weight)
        made = (gg, gu, gd, mixed, gtok, gcomb)
        gg, gu, gd, mixed, gtok, gcomb = pl.pallas_call(
            flush,
            out_shape=tuple(jax.ShapeDtypeStruct(m.shape, m.dtype) for m in made),
            in_specs=[held] * len(made),
            out_specs=[hbm] * len(made),
            scratch_shapes=[dma((len(made),))],
        )(*[pltpu.with_memory_space_constraint(m, pltpu.VMEM) for m in made])
        return mixed, gtok, gcomb.T, gg, gu, gd

    return jax.shard_map(
        step,
        mesh=mesh,
        in_specs=(
            P("ep", None),
            P("ep", None),
            P("ep", None),
            P("ep", None),
            P(None, ("ep", "tp")),
            P(None, ("ep", "tp")),
            P(("ep", "tp"), None),
        ),
        out_specs=(
            P("ep", None),
            P("ep", None),
            P("ep", None),
            P(None, ("ep", "tp")),
            P(None, ("ep", "tp")),
            P(("ep", "tp"), None),
        ),
        check_vma=False,
    )
```

```python
import functools

import jax
import jax.numpy as jnp
from jax import lax
from jax.experimental import pallas as pl
from jax.experimental.pallas import tpu as pltpu
from jax.sharding import PartitionSpec as P

CAP = 6
CORES = 2
MESH = pl.DeviceIdType.MESH
F32 = jnp.float32
BF16 = jnp.bfloat16


def dot_nn(a, b):
    return jnp.dot(a, b, preferred_element_type=F32)


def dot_nt(a, b):
    return lax.dot_general(a, b, (((1,), (1,)), ((), ())), preferred_element_type=F32)


def dot_tn(a, b):
    return lax.dot_general(a, b, (((0,), (0,)), ((), ())), preferred_element_type=F32)


def kernel(
    dims,
    ids_ref, comb_ref, tok_hbm, go_hbm, gate_hbm, up_hbm, down_hbm,
    mixed_ref, gtok_ref, gcomb_ref, gg_ref, gu_ref, gd_ref,
    xg, part, xs, xr, ys, yr, res,
    slab_out, slab_in, fin, fsc, pick, src, gos, wgu, wd, hid, dgu, pre_ref, dh_ref,
    w_sem, t_sem, za_s, za_r, zb_s, zb_r, gx, gy, g_send, d_send, d_recv,
    p_send, p_recv, rx_s, rx_r, ry_s, ry_r, f_s, f_r,
):
    NX, NY, NZ, CAPA = dims
    PIECE = NZ * CAPA
    TOKB, D = tok_hbm.shape
    SL = D // NX
    HS = SL // 2
    ROWS = NY * PIECE
    PER = NX * NY
    HID = wd.shape[1] // 2

    ep, tp = lax.axis_index("ep"), lax.axis_index("tp")
    c, x = lax.rem(tp, CORES), lax.div(tp, CORES)
    y, z = lax.rem(ep, NY), lax.div(ep, NY)

    def wx(v):
        return lax.rem(v + 2 * NX, NX)

    def wy(v):
        return lax.rem(v + 2 * NY, NY)

    def at(xx, yy, zz, cc):
        return (zz * NY + yy, xx * CORES + cc)

    yup, ydown = at(x, wy(y + 1), z, c), at(x, wy(y - 1), z, c)
    sibling = at(x, y, z, 1 - c)

    def remote(src, dst, ssem, rsem, device):
        return pltpu.make_async_remote_copy(
            src_ref=src, dst_ref=dst, send_sem=ssem, recv_sem=rsem,
            device_id=device, device_id_type=MESH,
        )

    def arrived(dst, rsem):
        remote(dst, dst, rsem, rsem, sibling).wait_recv()

    def sent(src, ssem):
        remote(src, src, ssem, ssem, sibling).wait_send()

    barrier = pltpu.get_barrier_semaphore()
    peers_z = [at(x, y, lax.rem(z + d, NZ), c) for d in range(1, NZ)]
    NT = NX * CORES
    peers_t = [(ep, lax.rem(tp + d, NT)) for d in range(1, NT)]
    far_up, far_down = at(x, wy(y + 2), z, c), at(x, wy(y - 2), z, c)
    partners = peers_z + peers_t + [yup, ydown, far_up, far_down]
    ynear, yfar = (yup, ydown), (far_up, far_down)
    xdev = [at(wx(x + k), y, z, c) for k in (2, 1, NX - 1)]
    for device in partners:
        pl.semaphore_signal(barrier, inc=1, device_id=device, device_id_type=MESH)

    features = pl.ds(pl.multiple_of(x * SL, 128), SL)

    @pl.when(c == 0)
    def _():
        pltpu.make_async_copy(tok_hbm, src, t_sem.at[0]).start()

    @pl.when(c == 1)
    def _():
        pltpu.make_async_copy(go_hbm, src, t_sem.at[0]).start()

    load_go = pltpu.make_async_copy(go_hbm.at[:, features], gos, t_sem.at[1])
    load_go.start()
    own_units, sib_units = (pl.ds(0, HID), pl.ds(HID, HID))
    own_pair, sib_pair = (pl.ds(0, 2 * HID), pl.ds(2 * HID, 2 * HID))
    loads = []
    for i in range(NX):
        rows = pl.ds(i * SL, SL)
        loads.append(pltpu.make_async_copy(gate_hbm.at[rows, :], wgu.at[i, :, pl.ds(0, HID)], w_sem.at[3 * i]))
        loads.append(pltpu.make_async_copy(up_hbm.at[rows, :], wgu.at[i, :, pl.ds(HID, HID)], w_sem.at[3 * i + 1]))
        loads.append(pltpu.make_async_copy(down_hbm.at[:, rows], wd.at[i, own_units], w_sem.at[3 * i + 2]))
    for load in loads:
        load.start()

    lane = lax.broadcasted_iota(jnp.int32, (TOKB, NZ * 16), 1)
    expert, place = lax.shift_right_logical(lane, 4), lane & 15
    diagonal = lax.broadcasted_iota(jnp.int32, (TOKB, TOKB), 0) == lax.broadcasted_iota(jnp.int32, (TOKB, TOKB), 1)

    def column(ref, k):
        return jnp.sum(jnp.where(diagonal, ref[k : k + 1, :].astype(F32), 0.0), axis=1, keepdims=True)

    id0, id1 = column(ids_ref, 0).astype(jnp.int32), column(ids_ref, 1).astype(jnp.int32)
    cw0, cw1 = column(comb_ref, 0), column(comb_ref, 1)
    is0, is1 = id0 == expert, id1 == expert
    named = jnp.where(is0 | is1, 1.0, 0.0)
    earlier = jnp.where(
        lax.broadcasted_iota(jnp.int32, (TOKB, TOKB), 0) > lax.broadcasted_iota(jnp.int32, (TOKB, TOKB), 1), 1.0, 0.0
    )
    rank = dot_nn(earlier.astype(BF16), named.astype(BF16)).astype(jnp.int32)
    hit0 = rank == place
    hit1 = (rank + CAPA == place) & (rank < CAPA)
    hit0 = hit0 & (place < CAPA)
    for g, mask in enumerate((is0 & hit0, is1 & hit0, is0 & hit1, is1 & hit1)):
        pick[g * TOKB : (g + 1) * TOKB, :] = jnp.where(mask, 1.0, 0.0).astype(BF16)

    one = jnp.ones((TOKB, 1), F32)
    w0 = jnp.where(c == 0, one, cw0)
    w1 = jnp.where(c == 0, one, cw1)
    spans = (slice(0, HS), slice(HS, SL))
    pltpu.make_async_copy(go_hbm, src, t_sem.at[0]).wait()
    far_first = [NZ // 2] + [d for k in range(NZ // 2 - 1, 0, -1) for d in (k, NZ - k)]
    xorder = [x, wx(x - 1), wx(x + 1), wx(x + 2)]

    def make_slabs(j):
        sources = []
        for h in range(2):
            span = pl.ds(pl.multiple_of(xorder[j] * SL + h * HS, 128), HS)
            v = src[:, span].astype(F32)
            sources += [(v * w0).astype(BF16), (v * w1).astype(BF16)]
        slabs = dot_tn(pick[...], jnp.concatenate(sources, axis=0)).astype(BF16)
        for e in range(NZ):
            slab_out[j, e] = slabs[e * 16 : (e + 1) * 16]
        slab_in[j, z] = slab_out[j, z]

    make_slabs(0)

    pl.semaphore_wait(barrier, len(partners))

    def give_weights():
        for load in loads:
            load.wait()

        @pl.when(c == 0)
        def _():
            remote(wgu.at[:, :, own_pair], wgu.at[:, :, sib_pair], p_send.at[0], p_recv.at[0], sibling).start()

        @pl.when(c == 1)
        def _():
            remote(wd.at[:, own_units], wd.at[:, sib_units], p_send.at[0], p_recv.at[0], sibling).start()

    def start_z(which, s_sem, r_sem):
        for d in far_first:
            remote(
                slab_out.at[which, lax.rem(z + d, NZ)], slab_in.at[which, z],
                s_sem.at[d], r_sem.at[d], peers_z[d - 1],
            ).start()

    def end_z(which, r_sem):
        for d in range(1, NZ):
            arrived(slab_in.at[which, lax.rem(z - d + NZ, NZ)], r_sem.at[d])

    start_z(0, za_s.at[0], za_r.at[0])

    @pl.when(c == 1)
    def _():
        for j in range(1, NX):
            make_slabs(j)
            start_z(j, za_s.at[j], za_r.at[j])

    give_weights()
    end_z(0, za_r.at[0])

    row = lax.broadcasted_iota(jnp.int32, (PIECE, NZ * 16), 0)
    col = lax.broadcasted_iota(jnp.int32, (PIECE, NZ * 16), 1)
    block, inner = lax.shift_right_logical(col, 4), col & 15
    tidy0 = jnp.where((block * CAPA + inner == row) & (inner < CAPA), 1.0, 0.0).astype(BF16)
    tidy1 = jnp.where(
        (block * CAPA + inner - CAPA == row) & (inner >= CAPA) & (inner < 2 * CAPA), 1.0, 0.0
    ).astype(BF16)

    def settle(j):
        got = slab_in[j].reshape(NZ * 16, HS)
        mine = c * PER + xorder[j] * NY + y
        xg[mine, :, 0:HS] = dot_nn(tidy0, got).astype(BF16)
        xg[mine, :, HS:SL] = dot_nn(tidy1, got).astype(BF16)

    settle(0)

    halves = (pl.ds(0, HS), pl.ds(HS, HS))
    HY = NY // 2
    order = (0, -1, 1, -2, 2, -3, 3, HY)

    def to_sibling(p):
        remote(xg.at[p], xg.at[p], d_send, d_recv, sibling).start()

    def send(ref, sem, device):
        remote(ref, ref, g_send, sem, device).start()

    def along_x(p, i):
        for k in range(NX - 1):
            send(xg.at[p], gx.at[k, i], xdev[k])

    def from_x(k):
        return wx(x - (2, 1, -1)[k])

    def begin_y(j, p, short):
        for d in range(2):
            if short:
                send(xg.at[p], gy.at[j, d, 1], yfar[d])
            send(xg.at[p], gy.at[j, d, 0], ynear[d])

    def onward_y(j, d, s, piece_at, short):
        p = piece_at(wy(y - s - 1 if d == 0 else y + s + 1))
        if s == HY - 1:
            arrived(xg.at[p, :, halves[d]], gy.at[j, d, s])
            return p
        arrived(xg.at[p], gy.at[j, d, s])
        if s == 0 and not short:
            send(xg.at[p], gy.at[j, d, 1], ynear[d])
        chain = j < 2 and not short
        if s == 1:
            send(xg.at[p], gy.at[j, d, 2], ynear[d])
        if s == (2 if chain else 1):
            send(xg.at[p, :, halves[d]], gy.at[j, d, 3], ynear[d] if chain else yfar[d])
        return p

    def gather_y_then_x():
        def piece_at(yy):
            return x * NY + yy

        p = piece_at(y)
        begin_y(0, p, True)
        along_x(p, 0)
        to_sibling(p)
        for s in range(HY):
            for d in range(2):
                p = onward_y(0, d, s, piece_at, True)
                if s < HY - 1 or d == 1:
                    along_x(p, 2 * s + 1 if s == HY - 1 else 2 * s + 1 + d)
                    to_sibling(p)
        for i in range(NY):
            for k in range(NX - 1):
                p = from_x(k) * NY + wy(y + order[i])
                arrived(xg.at[p], gx.at[k, i])
                to_sibling(p)

    def gather_y():
        def piece_of(xx):
            return lambda yy: PER + xx * NY + yy

        streams = [(j, piece_of(xorder[j])) for j in range(NX)]
        for j, piece_at in streams:
            if j:
                end_z(j, za_r.at[j])
                settle(j)
            begin_y(j, piece_at(y), False)
            to_sibling(piece_at(y))
        for s in range(HY):
            for j, piece_at in streams:
                for d in range(2):
                    p = onward_y(j, d, s, piece_at, False)
                    if s < HY - 1 or d == 1:
                        to_sibling(p)

    pl.when(c == 0)(gather_y_then_x)
    pl.when(c == 1)(gather_y)

    def rows_of(a, i):
        return xg[a * PER + i * NY : a * PER + (i + 1) * NY].reshape(ROWS, SL)

    def products(which):
        if which == 0:
            v = dot_nn(rows_of(0, 0), wgu[0, :, own_pair])
            for i in range(1, NX):
                v = v + dot_nn(rows_of(0, i), wgu[i, :, own_pair])
            pre_ref[...] = v
        else:
            v = dot_nt(rows_of(1, 0), wd[0, own_units])
            for i in range(1, NX):
                v = v + dot_nt(rows_of(1, i), wd[i, own_units])
            dh_ref[...] = v

    for when, which in ((0, 0), (1, 1)):
        pl.when(c == when)(functools.partial(products, which))
    arrived(xg.at[pl.ds((1 - c) * PER, PER)], d_recv)
    for when, which in ((0, 1), (1, 0)):
        pl.when(c == when)(functools.partial(products, which))
    pre, d_hidden = pre_ref[...], dh_ref[...]
    gate_pre, up_pre = pre[:, :HID], pre[:, HID:]
    sigma = jax.nn.sigmoid(gate_pre)
    silu = gate_pre * sigma
    hid[:, own_units] = (silu * up_pre).astype(BF16)
    dgu[:, pl.ds(0, HID)] = (d_hidden * up_pre * sigma * (1.0 + gate_pre * (1.0 - sigma))).astype(BF16)
    dgu[:, pl.ds(HID, HID)] = (d_hidden * silu).astype(BF16)

    @pl.when(c == 0)
    def _():
        remote(dgu.at[:, own_pair], dgu.at[:, sib_pair], p_send.at[1], p_recv.at[1], sibling).start()

    @pl.when(c == 1)
    def _():
        remote(hid.at[:, own_units], hid.at[:, sib_units], p_send.at[1], p_recv.at[1], sibling).start()

    def weight_grads(first, last):
        def step(i, carry):
            rows_x = xg[pl.ds(i * NY, NY)].reshape(ROWS, SL)
            rows_g = xg[pl.ds(PER + i * NY, NY)].reshape(ROWS, SL)
            both = dot_tn(rows_x, dgu[:, own_pair])
            span = pl.ds(pl.multiple_of(i * SL, 128), SL)
            gg_ref[span, :] = both[:, :HID].astype(BF16)
            gu_ref[span, :] = both[:, HID:].astype(BF16)
            gd_ref[:, span] = dot_tn(hid[:, own_units], rows_g).astype(BF16)
            return carry

        lax.fori_loop(first, last, step, 0)

    weight_grads(0, NX // 2)

    def expert_out_chunk(j):
        xx = wx(x + 2 - j)
        part[pl.ds(xx * NY, NY)] = dot_nn(hid[...], wd[xx]).reshape(NY, PIECE, SL)

    def input_grad_chunk(j):
        xx = wx(x + 2 - j)
        part[pl.ds(xx * NY, NY)] = dot_nt(dgu[...], wgu[xx]).reshape(NY, PIECE, SL)

    def own(p):
        return part[p]

    def y_out(j, d, s, v):
        out, into = ys.at[j, d, s], yr.at[j, d, s]
        if s == HY - 1:
            out, into = out.at[:, halves[d]], into.at[:, halves[d]]
            v = v[:, :HS] if d == 0 else v[:, HS:]
        out[...] = v.astype(BF16)
        hop = yfar if s == HY - 1 or (s == 1 and c_short[0]) else ynear
        remote(out, into, ry_s.at[j, d, s], ry_r.at[j, d, s], hop[d]).start()

    def y_came(j, d, s):
        into = yr.at[j, d, s]
        if s == HY - 1:
            into = into.at[:, halves[d]]
        arrived(into, ry_r.at[j, d, s])
        return into[...].astype(F32)

    def y_first(j, get):
        for d in range(2):
            y_out(j, d, 2, get(3 - 6 * d))
        v = get(HY)
        for d in range(2):
            y_out(j, d, 3, v)

    def y_second(j, d, get):
        v = get(2 - 4 * d) + y_came(j, d, 2)
        half = y_came(j, d, 3)
        lo, hi = v[:, :HS], v[:, HS:]
        lo, hi = (lo + half, hi) if d == 0 else (lo, hi + half)
        y_out(j, d, 1, jnp.concatenate([lo, hi], axis=1))

    def x_out(k, i, v):
        xs[k, i] = v.astype(BF16)
        remote(xs.at[k, i], xr.at[k, i], rx_s.at[k, i], rx_r.at[k, i], xdev[k]).start()

    def x_came(i):
        v = None
        for k in range(NX - 1):
            arrived(xr.at[k, i], rx_r.at[k, i])
            w = xr[k, i].astype(F32)
            v = w if v is None else v + w
        return v

    c_short = [False]
    back_order = (3, -3, HY, 2, -2, 1, -1, 0)
    chunk_of = (0, 1, 3)
    chunk_order = chunk_of + (2,)

    def at_y(off):
        return wy(y + off)

    def begin_x_then_y():
        arrived(wd.at[:, sib_units], p_recv.at[0])
        arrived(hid.at[:, sib_units], p_recv.at[1])
        for j in chunk_of:
            expert_out_chunk(j)
        for i, off in enumerate(back_order):
            for k in range(NX - 1):
                x_out(k, i, own(wx(x + 2 - chunk_of[k]) * NY + at_y(off)))
        expert_out_chunk(2)

    def begin_y_then_x():
        arrived(wgu.at[:, :, sib_pair], p_recv.at[0])
        arrived(dgu.at[:, sib_pair], p_recv.at[1])
        for j in chunk_order:
            input_grad_chunk(j)
            y_first(j, lambda off: own(wx(x + 2 - j) * NY + at_y(off)))

    pl.when(c == 0)(begin_x_then_y)
    pl.when(c == 1)(begin_y_then_x)

    weight_grads(NX // 2, NX)

    def end_x_then_y():
        c_short[0] = True

        def get(off):
            return own(x * NY + at_y(off)) + x_came(back_order.index(off))

        y_first(0, get)
        for d in range(2):
            y_second(0, d, get)
        for d in range(2):
            y_out(0, d, 0, get(1 - 2 * d))
        v = get(0)
        for s in range(2):
            for d in range(2):
                v = v + y_came(0, d, s)
        res[x] = v

    def end_y_then_x():
        c_short[0] = False

        def get(j):
            return lambda off: own(wx(x + 2 - j) * NY + at_y(off))

        for j in chunk_order:
            for d in range(2):
                y_second(j, d, get(j))
        for j in chunk_order:
            for d in range(2):
                y_out(j, d, 0, get(j)(1 - 2 * d) + y_came(j, d, 1))
        for j in chunk_order:
            v = get(j)(0) + y_came(j, 0, 0) + y_came(j, 1, 0)
            if j in chunk_of:
                x_out(chunk_of.index(j), 0, v)
            else:
                res[x] = v
        res[x] = res[x] + x_came(0)

    pl.when(c == 0)(end_x_then_y)
    pl.when(c == 1)(end_y_then_x)

    done = res[x].astype(BF16)
    back = (dot_tn(tidy0, done[:, :HS]) + dot_tn(tidy1, done[:, HS:])).astype(BF16)
    for e in range(NZ):
        slab_out[NX, e] = back[e * 16 : (e + 1) * 16]
    slab_in[NX, z] = slab_out[NX, z]
    start_z(NX, zb_s, zb_r)
    end_z(NX, zb_r)
    chosen = dot_nn(pick[...], slab_in[NX].reshape(NZ * 16, HS))
    c0 = jnp.where(c == 0, cw0, one)
    c1 = jnp.where(c == 0, cw1, one)
    scores = [jnp.zeros((TOKB, 1), F32), jnp.zeros((TOKB, 1), F32)]
    load_go.wait()
    for h, span in enumerate(spans):
        first = chosen[2 * h * TOKB : (2 * h + 1) * TOKB]
        second = chosen[(2 * h + 1) * TOKB : (2 * h + 2) * TOKB]
        fin[tp, :, h * HS : (h + 1) * HS] = (c0 * first + c1 * second).astype(BF16)
        g = gos[:, span].astype(F32)
        scores[0] = scores[0] + jnp.sum(g * first, axis=1, keepdims=True)
        scores[1] = scores[1] + jnp.sum(g * second, axis=1, keepdims=True)
    lane = lax.broadcasted_iota(jnp.int32, (TOKB, 128), 1)
    fsc[tp] = jnp.where(lane == 0, scores[0], jnp.where(lane == 1, scores[1], 0.0))

    for d in [NT // 2] + [d for k in range(NT // 2 - 1, 0, -1) for d in (k, NT - k)]:
        remote(fin.at[tp], fin.at[tp], f_s.at[0, d], f_r.at[0, d], peers_t[d - 1]).start()
        remote(fsc.at[tp], fsc.at[tp], f_s.at[1, d], f_r.at[1, d], peers_t[d - 1]).start()
    for d in range(1, NT):
        source = lax.rem(tp - d + NT, NT)
        arrived(fin.at[source], f_r.at[0, d])
        arrived(fsc.at[source], f_r.at[1, d])
    total_score = fsc[0]
    for i in range(NX):
        mixed_ref[:, i * SL : (i + 1) * SL] = fin[CORES * i]
        gtok_ref[:, i * SL : (i + 1) * SL] = fin[CORES * i + 1]
        if i:
            total_score = total_score + fsc[CORES * i]
    for k in range(2):
        gcomb_ref[k : k + 1, :] = jnp.sum(jnp.where(diagonal, total_score[:, k : k + 1], 0.0), axis=0, keepdims=True)

    for d in range(1, NZ):
        sent(slab_out.at[0, 0], za_s.at[0, d])
        sent(slab_out.at[0, 0], zb_s.at[d])
    for d in range(1, NT):
        sent(fin.at[tp], f_s.at[0, d])
        sent(fsc.at[tp], f_s.at[1, d])
    sent(xg.at[pl.ds(c * PER, PER)], d_send)

    def y_sent(j):
        for d in range(2):
            sent(ys.at[j, d, HY - 1].at[:, halves[d]], ry_s.at[j, d, HY - 1])
            for t in range(HY - 1):
                sent(ys.at[j, d, t], ry_s.at[j, d, t])

    @pl.when(c == 0)
    def _():
        sent(xg.at[pl.ds(0, PER - 1)], g_send)
        sent(wgu.at[:, :, own_pair], p_send.at[0])
        sent(dgu.at[:, own_pair], p_send.at[1])
        for k in range(NX - 1):
            for i in range(NY):
                sent(xs.at[k, i], rx_s.at[k, i])
        y_sent(0)

    @pl.when(c == 1)
    def _():
        sent(xg.at[pl.ds(0, PER - NX)], g_send)
        for j in range(1, NX):
            for d in range(1, NZ):
                sent(slab_out.at[0, 0], za_s.at[j, d])
        sent(wd.at[:, own_units], p_send.at[0])
        sent(hid.at[:, own_units], p_send.at[1])
        for k in range(NX - 1):
            sent(xs.at[k, 0], rx_s.at[k, 0])
        for j in range(NX):
            y_sent(j)


def flush(*refs):
    n = len(refs) // 2
    sems = refs[-1]
    copies = [pltpu.make_async_copy(refs[i], refs[n + i], sems.at[i]) for i in range(n)]
    for copy in copies:
        copy.start()
    for copy in copies:
        copy.wait()


def solution(mesh, cap=CAP, planes=8):
    NT = mesh.shape["tp"]
    NX, NZ = NT // CORES, planes
    NY = mesh.shape["ep"] // NZ

    def step(tokens, expert_ids, combine, grad_out, gate_weight, up_weight, down_weight):
        tokb, d = tokens.shape
        hidden = gate_weight.shape[1]
        sl, piece, per = d // NX, NZ * cap, NX * NY
        hs, rows, half_y = sl // 2, NY * piece, NY // 2
        dma, vmem, hbm = pltpu.SemaphoreType.DMA, pltpu.VMEM, pl.BlockSpec(memory_space=pl.ANY)
        held = pl.BlockSpec(memory_space=pltpu.VMEM)
        mixed, gtok, gcomb, gg, gu, gd = pl.pallas_call(
            functools.partial(kernel, (NX, NY, NZ, cap)),
            out_shape=(
                vmem((tokb, d), BF16),
                vmem((tokb, d), BF16),
                vmem(combine.shape[::-1], F32),
                vmem(gate_weight.shape, BF16),
                vmem(up_weight.shape, BF16),
                vmem(down_weight.shape, BF16),
            ),
            in_specs=[held] * 2 + [hbm] * 5,
            out_specs=[held] * 6,
            scratch_shapes=[
                vmem((2 * per, piece, sl), BF16),
                vmem((per, piece, sl), F32),
                vmem((NX - 1, NY, piece, sl), BF16),
                vmem((NX - 1, NY, piece, sl), BF16),
                vmem((NX, 2, half_y, piece, sl), BF16),
                vmem((NX, 2, half_y, piece, sl), BF16),
                vmem((NX, piece, sl), F32),
                vmem((NX + 1, NZ, 16, hs), BF16),
                vmem((NX + 1, NZ, 16, hs), BF16),
                vmem((NT, tokb, sl), BF16),
                vmem((NT, tokb, 128), F32),
                vmem((4 * tokb, NZ * 16), BF16),
                vmem((tokb, d), BF16), vmem((tokb, sl), BF16),
                vmem((NX, sl, 4 * hidden), BF16),
                vmem((NX, 2 * hidden, sl), BF16),
                vmem((rows, 2 * hidden), BF16),
                vmem((rows, 4 * hidden), BF16),
                vmem((rows, 2 * hidden), F32), vmem((rows, hidden), F32),
                dma((3 * NX,)), dma((2,)),
                dma((NX, NZ)), dma((NX, NZ)), dma((NZ,)), dma((NZ,)),
                dma((NX - 1, NY)), dma((NX, 2, half_y)),
                dma(()), dma(()), dma(()),
                dma((2,)), dma((2,)),
                dma((NX - 1, NY)), dma((NX - 1, NY)),
                dma((NX, 2, half_y)), dma((NX, 2, half_y)),
                dma((2, NT)), dma((2, NT)),
            ],
            compiler_params=pltpu.CompilerParams(
                collective_id=0, has_side_effects=True, vmem_limit_bytes=56 * 2**20
            ),
        )(expert_ids.T, combine.T, tokens, grad_out, gate_weight, up_weight, down_weight)
        made = (gg, gu, gd, mixed, gtok, gcomb)
        gg, gu, gd, mixed, gtok, gcomb = pl.pallas_call(
            flush,
            out_shape=tuple(jax.ShapeDtypeStruct(m.shape, m.dtype) for m in made),
            in_specs=[held] * len(made),
            out_specs=[hbm] * len(made),
            scratch_shapes=[dma((len(made),))],
        )(*[pltpu.with_memory_space_constraint(m, pltpu.VMEM) for m in made])
        return mixed, gtok, gcomb.T, gg, gu, gd

    return jax.shard_map(
        step,
        mesh=mesh,
        in_specs=(
            P("ep", None),
            P("ep", None),
            P("ep", None),
            P("ep", None),
            P(None, ("ep", "tp")),
            P(None, ("ep", "tp")),
            P(("ep", "tp"), None),
        ),
        out_specs=(
            P("ep", None),
            P("ep", None),
            P("ep", None),
            P(None, ("ep", "tp")),
            P(None, ("ep", "tp")),
            P(("ep", "tp"), None),
        ),
        check_vma=False,
    )
```

```python
import functools

import jax
import jax.numpy as jnp
from jax import lax
from jax.experimental import pallas as pl
from jax.experimental.pallas import tpu as pltpu
from jax.sharding import PartitionSpec as P

CAP = 6
CORES = 2
MESH = pl.DeviceIdType.MESH
F32 = jnp.float32
BF16 = jnp.bfloat16


def dot_nn(a, b):
    return jnp.dot(a, b, preferred_element_type=F32)


def dot_nt(a, b):
    return lax.dot_general(a, b, (((1,), (1,)), ((), ())), preferred_element_type=F32)


def dot_tn(a, b):
    return lax.dot_general(a, b, (((0,), (0,)), ((), ())), preferred_element_type=F32)


def kernel(
    dims,
    ids_ref, comb_ref, tok_hbm, go_hbm, gate_hbm, up_hbm, down_hbm,
    mixed_ref, gtok_ref, gcomb_ref, gg_ref, gu_ref, gd_ref,
    xg, part, xs, xr, ys, yr, res,
    slab_out, slab_in, fin, fsc, pick, src, gos, wgu, wd, hid, dgu, pre_ref, dh_ref,
    w_sem, t_sem, za_s, za_r, zb_s, zb_r, gx, gy, g_send, d_send, d_recv,
    p_send, p_recv, rx_s, rx_r, ry_s, ry_r, f_s, f_r,
):
    NX, NY, NZ, CAPA = dims
    PIECE = NZ * CAPA
    TOKB, D = tok_hbm.shape
    SL = D // NX
    HS = SL // 2
    ROWS = NY * PIECE
    PER = NX * NY
    HID = wd.shape[1] // 2

    ep, tp = lax.axis_index("ep"), lax.axis_index("tp")
    c, x = lax.rem(tp, CORES), lax.div(tp, CORES)
    y, z = lax.rem(ep, NY), lax.div(ep, NY)

    def wx(v):
        return lax.rem(v + 2 * NX, NX)

    def wy(v):
        return lax.rem(v + 2 * NY, NY)

    def at(xx, yy, zz, cc):
        return (zz * NY + yy, xx * CORES + cc)

    yup, ydown = at(x, wy(y + 1), z, c), at(x, wy(y - 1), z, c)
    sibling = at(x, y, z, 1 - c)

    def remote(src, dst, ssem, rsem, device):
        return pltpu.make_async_remote_copy(
            src_ref=src, dst_ref=dst, send_sem=ssem, recv_sem=rsem,
            device_id=device, device_id_type=MESH,
        )

    def arrived(dst, rsem):
        remote(dst, dst, rsem, rsem, sibling).wait_recv()

    def sent(src, ssem):
        remote(src, src, ssem, ssem, sibling).wait_send()

    barrier = pltpu.get_barrier_semaphore()
    peers_z = [at(x, y, lax.rem(z + d, NZ), c) for d in range(1, NZ)]
    NT = NX * CORES
    peers_t = [(ep, lax.rem(tp + d, NT)) for d in range(1, NT)]
    far_up, far_down = at(x, wy(y + 2), z, c), at(x, wy(y - 2), z, c)
    partners = peers_z + peers_t + [yup, ydown, far_up, far_down]
    ynear, yfar = (yup, ydown), (far_up, far_down)
    xdev = [at(wx(x + k), y, z, c) for k in (2, 1, NX - 1)]
    for device in partners:
        pl.semaphore_signal(barrier, inc=1, device_id=device, device_id_type=MESH)

    features = pl.ds(pl.multiple_of(x * SL, 128), SL)

    @pl.when(c == 0)
    def _():
        pltpu.make_async_copy(tok_hbm, src, t_sem.at[0]).start()

    @pl.when(c == 1)
    def _():
        pltpu.make_async_copy(go_hbm, src, t_sem.at[0]).start()

    load_go = pltpu.make_async_copy(go_hbm.at[:, features], gos, t_sem.at[1])
    load_go.start()
    own_units, sib_units = (pl.ds(0, HID), pl.ds(HID, HID))
    own_pair, sib_pair = (pl.ds(0, 2 * HID), pl.ds(2 * HID, 2 * HID))
    loads = []
    for i in range(NX):
        rows = pl.ds(i * SL, SL)
        loads.append(pltpu.make_async_copy(gate_hbm.at[rows, :], wgu.at[i, :, pl.ds(0, HID)], w_sem.at[3 * i]))
        loads.append(pltpu.make_async_copy(up_hbm.at[rows, :], wgu.at[i, :, pl.ds(HID, HID)], w_sem.at[3 * i + 1]))
        loads.append(pltpu.make_async_copy(down_hbm.at[:, rows], wd.at[i, own_units], w_sem.at[3 * i + 2]))
    for load in loads:
        load.start()

    lane = lax.broadcasted_iota(jnp.int32, (TOKB, NZ * 16), 1)
    expert, place = lax.shift_right_logical(lane, 4), lane & 15
    diagonal = lax.broadcasted_iota(jnp.int32, (TOKB, TOKB), 0) == lax.broadcasted_iota(jnp.int32, (TOKB, TOKB), 1)

    def column(ref, k):
        return jnp.sum(jnp.where(diagonal, ref[k : k + 1, :].astype(F32), 0.0), axis=1, keepdims=True)

    id0, id1 = column(ids_ref, 0).astype(jnp.int32), column(ids_ref, 1).astype(jnp.int32)
    cw0, cw1 = column(comb_ref, 0), column(comb_ref, 1)
    is0, is1 = id0 == expert, id1 == expert
    named = jnp.where(is0 | is1, 1.0, 0.0)
    earlier = jnp.where(
        lax.broadcasted_iota(jnp.int32, (TOKB, TOKB), 0) > lax.broadcasted_iota(jnp.int32, (TOKB, TOKB), 1), 1.0, 0.0
    )
    rank = dot_nn(earlier.astype(BF16), named.astype(BF16)).astype(jnp.int32)
    hit0 = rank == place
    hit1 = (rank + CAPA == place) & (rank < CAPA)
    hit0 = hit0 & (place < CAPA)
    for g, mask in enumerate((is0 & hit0, is1 & hit0, is0 & hit1, is1 & hit1)):
        pick[g * TOKB : (g + 1) * TOKB, :] = jnp.where(mask, 1.0, 0.0).astype(BF16)

    one = jnp.ones((TOKB, 1), F32)
    w0 = jnp.where(c == 0, one, cw0)
    w1 = jnp.where(c == 0, one, cw1)
    spans = (slice(0, HS), slice(HS, SL))
    pltpu.make_async_copy(go_hbm, src, t_sem.at[0]).wait()
    far_first = [NZ // 2] + [d for k in range(NZ // 2 - 1, 0, -1) for d in (k, NZ - k)]
    xorder = [x, wx(x - 1), wx(x + 1), wx(x + 2)]

    def make_slabs(j):
        sources = []
        for h in range(2):
            span = pl.ds(pl.multiple_of(xorder[j] * SL + h * HS, 128), HS)
            v = src[:, span].astype(F32)
            sources += [(v * w0).astype(BF16), (v * w1).astype(BF16)]
        slabs = dot_tn(pick[...], jnp.concatenate(sources, axis=0)).astype(BF16)
        for e in range(NZ):
            slab_out[j, e] = slabs[e * 16 : (e + 1) * 16]
        slab_in[j, z] = slab_out[j, z]

    make_slabs(0)

    pl.semaphore_wait(barrier, len(partners))

    def give_weights():
        for load in loads:
            load.wait()

        @pl.when(c == 0)
        def _():
            remote(wgu.at[:, :, own_pair], wgu.at[:, :, sib_pair], p_send.at[0], p_recv.at[0], sibling).start()

        @pl.when(c == 1)
        def _():
            remote(wd.at[:, own_units], wd.at[:, sib_units], p_send.at[0], p_recv.at[0], sibling).start()

    def start_z(which, s_sem, r_sem):
        for d in far_first:
            remote(
                slab_out.at[which, lax.rem(z + d, NZ)], slab_in.at[which, z],
                s_sem.at[d], r_sem.at[d], peers_z[d - 1],
            ).start()

    def end_z(which, r_sem):
        for d in range(1, NZ):
            arrived(slab_in.at[which, lax.rem(z - d + NZ, NZ)], r_sem.at[d])

    start_z(0, za_s.at[0], za_r.at[0])

    @pl.when(c == 1)
    def _():
        for j in range(1, NX):
            make_slabs(j)
            start_z(j, za_s.at[j], za_r.at[j])

    give_weights()
    end_z(0, za_r.at[0])

    row = lax.broadcasted_iota(jnp.int32, (PIECE, NZ * 16), 0)
    col = lax.broadcasted_iota(jnp.int32, (PIECE, NZ * 16), 1)
    block, inner = lax.shift_right_logical(col, 4), col & 15
    tidy0 = jnp.where((block * CAPA + inner == row) & (inner < CAPA), 1.0, 0.0).astype(BF16)
    tidy1 = jnp.where(
        (block * CAPA + inner - CAPA == row) & (inner >= CAPA) & (inner < 2 * CAPA), 1.0, 0.0
    ).astype(BF16)

    def settle(j):
        got = slab_in[j].reshape(NZ * 16, HS)
        mine = c * PER + xorder[j] * NY + y
        xg[mine, :, 0:HS] = dot_nn(tidy0, got).astype(BF16)
        xg[mine, :, HS:SL] = dot_nn(tidy1, got).astype(BF16)

    settle(0)

    halves = (pl.ds(0, HS), pl.ds(HS, HS))
    HY = NY // 2
    order = (0, -1, 1, -2, 2, -3, 3, HY)

    def to_sibling(p):
        remote(xg.at[p], xg.at[p], d_send, d_recv, sibling).start()

    def send(ref, sem, device):
        remote(ref, ref, g_send, sem, device).start()

    def along_x(p, i):
        for k in range(NX - 1):
            send(xg.at[p], gx.at[k, i], xdev[k])

    def from_x(k):
        return wx(x - (2, 1, -1)[k])

    def begin_y(j, p, short):
        for d in range(2):
            if short:
                send(xg.at[p], gy.at[j, d, 1], yfar[d])
            send(xg.at[p], gy.at[j, d, 0], ynear[d])

    def onward_y(j, d, s, piece_at, short):
        p = piece_at(wy(y - s - 1 if d == 0 else y + s + 1))
        if s == HY - 1:
            arrived(xg.at[p, :, halves[d]], gy.at[j, d, s])
            return p
        arrived(xg.at[p], gy.at[j, d, s])
        if s == 0 and not short:
            send(xg.at[p], gy.at[j, d, 1], ynear[d])
        chain = j < 2 and not short
        if s == 1:
            send(xg.at[p], gy.at[j, d, 2], ynear[d])
        if s == (2 if chain else 1):
            send(xg.at[p, :, halves[d]], gy.at[j, d, 3], ynear[d] if chain else yfar[d])
        return p

    def gather_y_then_x():
        def piece_at(yy):
            return x * NY + yy

        p = piece_at(y)
        begin_y(0, p, True)
        along_x(p, 0)
        to_sibling(p)
        for s in range(HY):
            for d in range(2):
                p = onward_y(0, d, s, piece_at, True)
                if s < HY - 1 or d == 1:
                    along_x(p, 2 * s + 1 if s == HY - 1 else 2 * s + 1 + d)
                    to_sibling(p)
        for i in range(NY):
            for k in range(NX - 1):
                p = from_x(k) * NY + wy(y + order[i])
                arrived(xg.at[p], gx.at[k, i])
                to_sibling(p)

    def gather_y():
        def piece_of(xx):
            return lambda yy: PER + xx * NY + yy

        streams = [(j, piece_of(xorder[j])) for j in range(NX)]
        for j, piece_at in streams:
            if j:
                end_z(j, za_r.at[j])
                settle(j)
            begin_y(j, piece_at(y), False)
            to_sibling(piece_at(y))
        for s in range(HY):
            if s == HY - 1:
                arrived(xg.at[pl.ds(0, PER)], d_recv)
                products(0)
                make_hidden()
                remote(hid.at[:, own_units], hid.at[:, sib_units], p_send.at[1], p_recv.at[1], sibling).start()
            for j, piece_at in streams:
                for d in range(2):
                    p = onward_y(j, d, s, piece_at, False)
                    if s < HY - 1 or d == 1:
                        to_sibling(p)


    def rows_of(a, i):
        return xg[a * PER + i * NY : a * PER + (i + 1) * NY].reshape(ROWS, SL)

    def products(which):
        if which == 0:
            v = dot_nn(rows_of(0, 0), wgu[0, :, own_pair])
            for i in range(1, NX):
                v = v + dot_nn(rows_of(0, i), wgu[i, :, own_pair])
            pre_ref[...] = v
        else:
            v = dot_nt(rows_of(1, 0), wd[0, own_units])
            for i in range(1, NX):
                v = v + dot_nt(rows_of(1, i), wd[i, own_units])
            dh_ref[...] = v

    def make_hidden():
        gate_pre, up_pre = pre_ref[:, :HID], pre_ref[:, HID:]
        hid[:, own_units] = (gate_pre * jax.nn.sigmoid(gate_pre) * up_pre).astype(BF16)

    def make_grads():
        gate_pre, up_pre, d_hidden = pre_ref[:, :HID], pre_ref[:, HID:], dh_ref[...]
        sigma = jax.nn.sigmoid(gate_pre)
        dgu[:, pl.ds(0, HID)] = (d_hidden * up_pre * sigma * (1.0 + gate_pre * (1.0 - sigma))).astype(BF16)
        dgu[:, pl.ds(HID, HID)] = (d_hidden * (gate_pre * sigma)).astype(BF16)

    def weight_grads(first, last):
        def step(i, carry):
            rows_x = xg[pl.ds(i * NY, NY)].reshape(ROWS, SL)
            rows_g = xg[pl.ds(PER + i * NY, NY)].reshape(ROWS, SL)
            both = dot_tn(rows_x, dgu[:, own_pair])
            span = pl.ds(pl.multiple_of(i * SL, 128), SL)
            gg_ref[span, :] = both[:, :HID].astype(BF16)
            gu_ref[span, :] = both[:, HID:].astype(BF16)
            gd_ref[:, span] = dot_tn(hid[:, own_units], rows_g).astype(BF16)
            return carry

        lax.fori_loop(first, last, step, 0)

    def expert_out_chunk(j):
        xx = wx(x + 2 - j)
        part[pl.ds(xx * NY, NY)] = dot_nn(hid[...], wd[xx]).reshape(NY, PIECE, SL)

    def input_grad_chunk(j):
        xx = wx(x + 2 - j)
        part[pl.ds(xx * NY, NY)] = dot_nt(dgu[...], wgu[xx]).reshape(NY, PIECE, SL)

    def own(p):
        return part[p]

    def y_out(j, d, s, v):
        out, into = ys.at[j, d, s], yr.at[j, d, s]
        if s == HY - 1:
            out, into = out.at[:, halves[d]], into.at[:, halves[d]]
            v = v[:, :HS] if d == 0 else v[:, HS:]
        out[...] = v.astype(BF16)
        hop = yfar if s == HY - 1 or (s == 1 and c_short[0]) else ynear
        remote(out, into, ry_s.at[j, d, s], ry_r.at[j, d, s], hop[d]).start()

    def y_came(j, d, s):
        into = yr.at[j, d, s]
        if s == HY - 1:
            into = into.at[:, halves[d]]
        arrived(into, ry_r.at[j, d, s])
        return into[...].astype(F32)

    def y_first(j, get):
        for d in range(2):
            y_out(j, d, 2, get(3 - 6 * d))
        v = get(HY)
        for d in range(2):
            y_out(j, d, 3, v)

    def y_second(j, d, get):
        v = get(2 - 4 * d) + y_came(j, d, 2)
        half = y_came(j, d, 3)
        lo, hi = v[:, :HS], v[:, HS:]
        lo, hi = (lo + half, hi) if d == 0 else (lo, hi + half)
        y_out(j, d, 1, jnp.concatenate([lo, hi], axis=1))

    def x_out(k, i, v):
        xs[k, i] = v.astype(BF16)
        remote(xs.at[k, i], xr.at[k, i], rx_s.at[k, i], rx_r.at[k, i], xdev[k]).start()

    def x_came(i):
        v = None
        for k in range(NX - 1):
            arrived(xr.at[k, i], rx_r.at[k, i])
            w = xr[k, i].astype(F32)
            v = w if v is None else v + w
        return v

    c_short = [False]
    back_order = (3, -3, HY, 2, -2, 1, -1, 0)
    chunk_of = (0, 1, 3)
    chunk_order = chunk_of + (2,)

    def at_y(off):
        return wy(y + off)

    def begin_x_then_y():
        arrived(wd.at[:, sib_units], p_recv.at[0])
        arrived(hid.at[:, sib_units], p_recv.at[1])
        for j in chunk_of:
            expert_out_chunk(j)
        for i, off in enumerate(back_order):
            for k in range(NX - 1):
                x_out(k, i, own(wx(x + 2 - chunk_of[k]) * NY + at_y(off)))
        expert_out_chunk(2)

    def begin_y_then_x():
        arrived(wgu.at[:, :, sib_pair], p_recv.at[0])
        arrived(dgu.at[:, sib_pair], p_recv.at[1])
        for j in chunk_order:
            input_grad_chunk(j)
            y_first(j, lambda off: own(wx(x + 2 - j) * NY + at_y(off)))

    @pl.when(c == 0)
    def _():
        gather_y_then_x()
        products(0)
        make_hidden()
        begin_x_then_y()
        arrived(xg.at[pl.ds(PER, PER)], d_recv)
        products(1)
        make_grads()
        remote(dgu.at[:, own_pair], dgu.at[:, sib_pair], p_send.at[1], p_recv.at[1], sibling).start()

    @pl.when(c == 1)
    def _():
        gather_y()
        products(1)
        make_grads()

    weight_grads(0, NX // 2)
    pl.when(c == 1)(begin_y_then_x)

    weight_grads(NX // 2, NX)

    def end_x_then_y():
        c_short[0] = True

        def get(off):
            return own(x * NY + at_y(off)) + x_came(back_order.index(off))

        y_first(0, get)
        for d in range(2):
            y_second(0, d, get)
        for d in range(2):
            y_out(0, d, 0, get(1 - 2 * d))
        v = get(0)
        for s in range(2):
            for d in range(2):
                v = v + y_came(0, d, s)
        res[x] = v

    def end_y_then_x():
        c_short[0] = False

        def get(j):
            return lambda off: own(wx(x + 2 - j) * NY + at_y(off))

        for j in chunk_order:
            for d in range(2):
                y_second(j, d, get(j))
        for j in chunk_order:
            for d in range(2):
                y_out(j, d, 0, get(j)(1 - 2 * d) + y_came(j, d, 1))
        for j in chunk_order:
            v = get(j)(0) + y_came(j, 0, 0) + y_came(j, 1, 0)
            if j in chunk_of:
                x_out(chunk_of.index(j), 0, v)
            else:
                res[x] = v
        res[x] = res[x] + x_came(0)

    pl.when(c == 0)(end_x_then_y)
    pl.when(c == 1)(end_y_then_x)

    done = res[x].astype(BF16)
    back = (dot_tn(tidy0, done[:, :HS]) + dot_tn(tidy1, done[:, HS:])).astype(BF16)
    for e in range(NZ):
        slab_out[NX, e] = back[e * 16 : (e + 1) * 16]
    slab_in[NX, z] = slab_out[NX, z]
    start_z(NX, zb_s, zb_r)
    end_z(NX, zb_r)
    chosen = dot_nn(pick[...], slab_in[NX].reshape(NZ * 16, HS))
    c0 = jnp.where(c == 0, cw0, one)
    c1 = jnp.where(c == 0, cw1, one)
    scores = [jnp.zeros((TOKB, 1), F32), jnp.zeros((TOKB, 1), F32)]
    load_go.wait()
    for h, span in enumerate(spans):
        first = chosen[2 * h * TOKB : (2 * h + 1) * TOKB]
        second = chosen[(2 * h + 1) * TOKB : (2 * h + 2) * TOKB]
        fin[tp, :, h * HS : (h + 1) * HS] = (c0 * first + c1 * second).astype(BF16)
        g = gos[:, span].astype(F32)
        scores[0] = scores[0] + jnp.sum(g * first, axis=1, keepdims=True)
        scores[1] = scores[1] + jnp.sum(g * second, axis=1, keepdims=True)
    lane = lax.broadcasted_iota(jnp.int32, (TOKB, 128), 1)
    fsc[tp] = jnp.where(lane == 0, scores[0], jnp.where(lane == 1, scores[1], 0.0))

    for d in [NT // 2] + [d for k in range(NT // 2 - 1, 0, -1) for d in (k, NT - k)]:
        remote(fin.at[tp], fin.at[tp], f_s.at[0, d], f_r.at[0, d], peers_t[d - 1]).start()
        remote(fsc.at[tp], fsc.at[tp], f_s.at[1, d], f_r.at[1, d], peers_t[d - 1]).start()
    for d in range(1, NT):
        source = lax.rem(tp - d + NT, NT)
        arrived(fin.at[source], f_r.at[0, d])
        arrived(fsc.at[source], f_r.at[1, d])
    total_score = fsc[0]
    for i in range(NX):
        mixed_ref[:, i * SL : (i + 1) * SL] = fin[CORES * i]
        gtok_ref[:, i * SL : (i + 1) * SL] = fin[CORES * i + 1]
        if i:
            total_score = total_score + fsc[CORES * i]
    for k in range(2):
        gcomb_ref[k : k + 1, :] = jnp.sum(jnp.where(diagonal, total_score[:, k : k + 1], 0.0), axis=0, keepdims=True)

    for d in range(1, NZ):
        sent(slab_out.at[0, 0], za_s.at[0, d])
        sent(slab_out.at[0, 0], zb_s.at[d])
    for d in range(1, NT):
        sent(fin.at[tp], f_s.at[0, d])
        sent(fsc.at[tp], f_s.at[1, d])
    sent(xg.at[pl.ds(c * PER, PER)], d_send)

    def y_sent(j):
        for d in range(2):
            sent(ys.at[j, d, HY - 1].at[:, halves[d]], ry_s.at[j, d, HY - 1])
            for t in range(HY - 1):
                sent(ys.at[j, d, t], ry_s.at[j, d, t])

    @pl.when(c == 0)
    def _():
        sent(xg.at[pl.ds(0, PER - 1)], g_send)
        sent(wgu.at[:, :, own_pair], p_send.at[0])
        sent(dgu.at[:, own_pair], p_send.at[1])
        for k in range(NX - 1):
            for i in range(NY):
                sent(xs.at[k, i], rx_s.at[k, i])
        y_sent(0)

    @pl.when(c == 1)
    def _():
        sent(xg.at[pl.ds(0, PER - NX)], g_send)
        for j in range(1, NX):
            for d in range(1, NZ):
                sent(slab_out.at[0, 0], za_s.at[j, d])
        sent(wd.at[:, own_units], p_send.at[0])
        sent(hid.at[:, own_units], p_send.at[1])
        for k in range(NX - 1):
            sent(xs.at[k, 0], rx_s.at[k, 0])
        for j in range(NX):
            y_sent(j)


def flush(*refs):
    n = len(refs) // 2
    sems = refs[-1]
    copies = [pltpu.make_async_copy(refs[i], refs[n + i], sems.at[i]) for i in range(n)]
    for copy in copies:
        copy.start()
    for copy in copies:
        copy.wait()


def solution(mesh, cap=CAP, planes=8):
    NT = mesh.shape["tp"]
    NX, NZ = NT // CORES, planes
    NY = mesh.shape["ep"] // NZ

    def step(tokens, expert_ids, combine, grad_out, gate_weight, up_weight, down_weight):
        tokb, d = tokens.shape
        hidden = gate_weight.shape[1]
        sl, piece, per = d // NX, NZ * cap, NX * NY
        hs, rows, half_y = sl // 2, NY * piece, NY // 2
        dma, vmem, hbm = pltpu.SemaphoreType.DMA, pltpu.VMEM, pl.BlockSpec(memory_space=pl.ANY)
        held = pl.BlockSpec(memory_space=pltpu.VMEM)
        mixed, gtok, gcomb, gg, gu, gd = pl.pallas_call(
            functools.partial(kernel, (NX, NY, NZ, cap)),
            out_shape=(
                vmem((tokb, d), BF16),
                vmem((tokb, d), BF16),
                vmem(combine.shape[::-1], F32),
                vmem(gate_weight.shape, BF16),
                vmem(up_weight.shape, BF16),
                vmem(down_weight.shape, BF16),
            ),
            in_specs=[held] * 2 + [hbm] * 5,
            out_specs=[held] * 6,
            scratch_shapes=[
                vmem((2 * per, piece, sl), BF16),
                vmem((per, piece, sl), F32),
                vmem((NX - 1, NY, piece, sl), BF16),
                vmem((NX - 1, NY, piece, sl), BF16),
                vmem((NX, 2, half_y, piece, sl), BF16),
                vmem((NX, 2, half_y, piece, sl), BF16),
                vmem((NX, piece, sl), F32),
                vmem((NX + 1, NZ, 16, hs), BF16),
                vmem((NX + 1, NZ, 16, hs), BF16),
                vmem((NT, tokb, sl), BF16),
                vmem((NT, tokb, 128), F32),
                vmem((4 * tokb, NZ * 16), BF16),
                vmem((tokb, d), BF16), vmem((tokb, sl), BF16),
                vmem((NX, sl, 4 * hidden), BF16),
                vmem((NX, 2 * hidden, sl), BF16),
                vmem((rows, 2 * hidden), BF16),
                vmem((rows, 4 * hidden), BF16),
                vmem((rows, 2 * hidden), F32), vmem((rows, hidden), F32),
                dma((3 * NX,)), dma((2,)),
                dma((NX, NZ)), dma((NX, NZ)), dma((NZ,)), dma((NZ,)),
                dma((NX - 1, NY)), dma((NX, 2, half_y)),
                dma(()), dma(()), dma(()),
                dma((2,)), dma((2,)),
                dma((NX - 1, NY)), dma((NX - 1, NY)),
                dma((NX, 2, half_y)), dma((NX, 2, half_y)),
                dma((2, NT)), dma((2, NT)),
            ],
            compiler_params=pltpu.CompilerParams(
                collective_id=0, has_side_effects=True, vmem_limit_bytes=56 * 2**20
            ),
        )(expert_ids.T, combine.T, tokens, grad_out, gate_weight, up_weight, down_weight)
        made = (gg, gu, gd, mixed, gtok, gcomb)
        gg, gu, gd, mixed, gtok, gcomb = pl.pallas_call(
            flush,
            out_shape=tuple(jax.ShapeDtypeStruct(m.shape, m.dtype) for m in made),
            in_specs=[held] * len(made),
            out_specs=[hbm] * len(made),
            scratch_shapes=[dma((len(made),))],
        )(*[pltpu.with_memory_space_constraint(m, pltpu.VMEM) for m in made])
        return mixed, gtok, gcomb.T, gg, gu, gd

    return jax.shard_map(
        step,
        mesh=mesh,
        in_specs=(
            P("ep", None),
            P("ep", None),
            P("ep", None),
            P("ep", None),
            P(None, ("ep", "tp")),
            P(None, ("ep", "tp")),
            P(("ep", "tp"), None),
        ),
        out_specs=(
            P("ep", None),
            P("ep", None),
            P("ep", None),
            P(None, ("ep", "tp")),
            P(None, ("ep", "tp")),
            P(("ep", "tp"), None),
        ),
        check_vma=False,
    )
```

```python
import functools

import jax
import jax.numpy as jnp
from jax import lax
from jax.experimental import pallas as pl
from jax.experimental.pallas import tpu as pltpu
from jax.sharding import PartitionSpec as P

CAP = 6
CORES = 2
MESH = pl.DeviceIdType.MESH
F32 = jnp.float32
BF16 = jnp.bfloat16


def dot_nn(a, b):
    return jnp.dot(a, b, preferred_element_type=F32)


def dot_nt(a, b):
    return lax.dot_general(a, b, (((1,), (1,)), ((), ())), preferred_element_type=F32)


def dot_tn(a, b):
    return lax.dot_general(a, b, (((0,), (0,)), ((), ())), preferred_element_type=F32)


def kernel(
    dims,
    ids_ref, comb_ref, tok_hbm, go_hbm, gate_hbm, up_hbm, down_hbm,
    mixed_ref, gtok_ref, gcomb_ref, gg_ref, gu_ref, gd_ref,
    xg, part, xs, xr, ys, yr, res,
    slab_out, slab_in, fin, fsc, pick, src, gos, wgu, wd, hid, dgu, pre_ref, dh_ref,
    w_sem, t_sem, za_s, za_r, zb_s, zb_r, gx, gy, g_send, d_send, d_recv,
    p_send, p_recv, rx_s, rx_r, ry_s, ry_r, f_s, f_r,
):
    NX, NY, NZ, CAPA = dims
    PIECE = NZ * CAPA
    TOKB, D = tok_hbm.shape
    SL = D // NX
    HS = SL // 2
    ROWS = NY * PIECE
    PER = NX * NY
    HID = wd.shape[1] // 2

    ep, tp = lax.axis_index("ep"), lax.axis_index("tp")
    c, x = lax.rem(tp, CORES), lax.div(tp, CORES)
    y, z = lax.rem(ep, NY), lax.div(ep, NY)

    def wx(v):
        return lax.rem(v + 2 * NX, NX)

    def wy(v):
        return lax.rem(v + 2 * NY, NY)

    def at(xx, yy, zz, cc):
        return (zz * NY + yy, xx * CORES + cc)

    yup, ydown = at(x, wy(y + 1), z, c), at(x, wy(y - 1), z, c)
    sibling = at(x, y, z, 1 - c)

    def remote(src, dst, ssem, rsem, device):
        return pltpu.make_async_remote_copy(
            src_ref=src, dst_ref=dst, send_sem=ssem, recv_sem=rsem,
            device_id=device, device_id_type=MESH,
        )

    def arrived(dst, rsem):
        remote(dst, dst, rsem, rsem, sibling).wait_recv()

    def sent(src, ssem):
        remote(src, src, ssem, ssem, sibling).wait_send()

    barrier = pltpu.get_barrier_semaphore()
    peers_z = [at(x, y, lax.rem(z + d, NZ), c) for d in range(1, NZ)]
    NT = NX * CORES
    peers_t = [(ep, lax.rem(tp + d, NT)) for d in range(1, NT)]
    far_up, far_down = at(x, wy(y + 2), z, c), at(x, wy(y - 2), z, c)
    partners = peers_z + peers_t + [yup, ydown, far_up, far_down]
    ynear, yfar = (yup, ydown), (far_up, far_down)
    xdev = [at(wx(x + k), y, z, c) for k in (2, 1, NX - 1)]
    for device in partners:
        pl.semaphore_signal(barrier, inc=1, device_id=device, device_id_type=MESH)

    features = pl.ds(pl.multiple_of(x * SL, 128), SL)

    @pl.when(c == 0)
    def _():
        pltpu.make_async_copy(tok_hbm, src, t_sem.at[0]).start()

    @pl.when(c == 1)
    def _():
        pltpu.make_async_copy(go_hbm, src, t_sem.at[0]).start()

    load_go = pltpu.make_async_copy(go_hbm.at[:, features], gos, t_sem.at[1])
    load_go.start()
    own_units, sib_units = (pl.ds(0, HID), pl.ds(HID, HID))
    own_pair, sib_pair = (pl.ds(0, 2 * HID), pl.ds(2 * HID, 2 * HID))
    loads = []
    for i in range(NX):
        rows = pl.ds(i * SL, SL)
        loads.append(pltpu.make_async_copy(gate_hbm.at[rows, :], wgu.at[i, :, pl.ds(0, HID)], w_sem.at[3 * i]))
        loads.append(pltpu.make_async_copy(up_hbm.at[rows, :], wgu.at[i, :, pl.ds(HID, HID)], w_sem.at[3 * i + 1]))
        loads.append(pltpu.make_async_copy(down_hbm.at[:, rows], wd.at[i, own_units], w_sem.at[3 * i + 2]))
    for load in loads:
        load.start()

    lane = lax.broadcasted_iota(jnp.int32, (TOKB, NZ * 16), 1)
    expert, place = lax.shift_right_logical(lane, 4), lane & 15
    diagonal = lax.broadcasted_iota(jnp.int32, (TOKB, TOKB), 0) == lax.broadcasted_iota(jnp.int32, (TOKB, TOKB), 1)

    def column(ref, k):
        return jnp.sum(jnp.where(diagonal, ref[k : k + 1, :].astype(F32), 0.0), axis=1, keepdims=True)

    id0, id1 = column(ids_ref, 0).astype(jnp.int32), column(ids_ref, 1).astype(jnp.int32)
    cw0, cw1 = column(comb_ref, 0), column(comb_ref, 1)
    is0, is1 = id0 == expert, id1 == expert
    named = jnp.where(is0 | is1, 1.0, 0.0)
    earlier = jnp.where(
        lax.broadcasted_iota(jnp.int32, (TOKB, TOKB), 0) > lax.broadcasted_iota(jnp.int32, (TOKB, TOKB), 1), 1.0, 0.0
    )
    rank = dot_nn(earlier.astype(BF16), named.astype(BF16)).astype(jnp.int32)
    hit0 = rank == place
    hit1 = (rank + CAPA == place) & (rank < CAPA)
    hit0 = hit0 & (place < CAPA)
    for g, mask in enumerate((is0 & hit0, is1 & hit0, is0 & hit1, is1 & hit1)):
        pick[g * TOKB : (g + 1) * TOKB, :] = jnp.where(mask, 1.0, 0.0).astype(BF16)

    one = jnp.ones((TOKB, 1), F32)
    w0 = jnp.where(c == 0, one, cw0)
    w1 = jnp.where(c == 0, one, cw1)
    spans = (slice(0, HS), slice(HS, SL))
    pltpu.make_async_copy(go_hbm, src, t_sem.at[0]).wait()
    far_first = [NZ // 2] + [d for k in range(NZ // 2 - 1, 0, -1) for d in (k, NZ - k)]
    xorder = [x, wx(x - 1), wx(x + 1), wx(x + 2)]

    def make_slabs(j):
        sources = []
        for h in range(2):
            span = pl.ds(pl.multiple_of(xorder[j] * SL + h * HS, 128), HS)
            v = src[:, span].astype(F32)
            sources += [(v * w0).astype(BF16), (v * w1).astype(BF16)]
        slabs = dot_tn(pick[...], jnp.concatenate(sources, axis=0)).astype(BF16)
        for e in range(NZ):
            slab_out[j, e] = slabs[e * 16 : (e + 1) * 16]
        slab_in[j, z] = slab_out[j, z]

    make_slabs(0)

    pl.semaphore_wait(barrier, len(partners))

    def give_weights():
        for load in loads:
            load.wait()

        @pl.when(c == 0)
        def _():
            remote(wgu.at[:, :, own_pair], wgu.at[:, :, sib_pair], p_send.at[0], p_recv.at[0], sibling).start()

        @pl.when(c == 1)
        def _():
            remote(wd.at[:, own_units], wd.at[:, sib_units], p_send.at[0], p_recv.at[0], sibling).start()

    def start_z(which, s_sem, r_sem):
        for d in far_first:
            remote(
                slab_out.at[which, lax.rem(z + d, NZ)], slab_in.at[which, z],
                s_sem.at[d], r_sem.at[d], peers_z[d - 1],
            ).start()

    def end_z(which, r_sem):
        for d in range(1, NZ):
            arrived(slab_in.at[which, lax.rem(z - d + NZ, NZ)], r_sem.at[d])

    start_z(0, za_s.at[0], za_r.at[0])

    @pl.when(c == 1)
    def _():
        for j in range(1, NX):
            make_slabs(j)
            start_z(j, za_s.at[j], za_r.at[j])

    give_weights()
    end_z(0, za_r.at[0])

    row = lax.broadcasted_iota(jnp.int32, (PIECE, NZ * 16), 0)
    col = lax.broadcasted_iota(jnp.int32, (PIECE, NZ * 16), 1)
    block, inner = lax.shift_right_logical(col, 4), col & 15
    tidy0 = jnp.where((block * CAPA + inner == row) & (inner < CAPA), 1.0, 0.0).astype(BF16)
    tidy1 = jnp.where(
        (block * CAPA + inner - CAPA == row) & (inner >= CAPA) & (inner < 2 * CAPA), 1.0, 0.0
    ).astype(BF16)

    def settle(j):
        got = slab_in[j].reshape(NZ * 16, HS)
        mine = c * PER + xorder[j] * NY + y
        xg[mine, :, 0:HS] = dot_nn(tidy0, got).astype(BF16)
        xg[mine, :, HS:SL] = dot_nn(tidy1, got).astype(BF16)

    settle(0)

    halves = (pl.ds(0, HS), pl.ds(HS, HS))
    HY = NY // 2
    order = (0, -1, 1, -2, 2, -3, 3, HY)
    RELAYED = 5

    def to_sibling(p):
        remote(xg.at[p], xg.at[p], d_send, d_recv, sibling).start()

    def send(ref, sem, device):
        remote(ref, ref, g_send, sem, device).start()

    def along_x(p, i):
        for k in range(1 if i < RELAYED else 0, NX - 1):
            send(xg.at[p], gx.at[k, i], xdev[k])

    def relay_x(i):
        for d, k in enumerate((1, 2)):
            p = from_x(k) * NY + wy(y + order[i])
            arrived(xg.at[p], gx.at[k, i])
            send(xg.at[p, :, halves[d]], gx.at[(0, NX - 1)[d], i], xdev[k])
            to_sibling(p)

    def from_x(k):
        return wx(x - (2, 1, -1)[k])

    def begin_y(j, p, short):
        for d in range(2):
            if short:
                send(xg.at[p], gy.at[j, d, 1], yfar[d])
            send(xg.at[p], gy.at[j, d, 0], ynear[d])

    def onward_y(j, d, s, piece_at, short):
        p = piece_at(wy(y - s - 1 if d == 0 else y + s + 1))
        if s == HY - 1:
            arrived(xg.at[p, :, halves[d]], gy.at[j, d, s])
            return p
        arrived(xg.at[p], gy.at[j, d, s])
        if s == 0 and not short:
            send(xg.at[p], gy.at[j, d, 1], ynear[d])
        chain = j < 2 and not short
        if s == 1:
            send(xg.at[p], gy.at[j, d, 2], ynear[d])
        if s == (2 if chain else 1):
            send(xg.at[p, :, halves[d]], gy.at[j, d, 3], ynear[d] if chain else yfar[d])
        return p

    def gather_y_then_x():
        def piece_at(yy):
            return x * NY + yy

        p = piece_at(y)
        begin_y(0, p, True)
        along_x(p, 0)
        to_sibling(p)
        for s in range(HY):
            for d in range(2):
                p = onward_y(0, d, s, piece_at, True)
                if s < HY - 1 or d == 1:
                    along_x(p, 2 * s + 1 if s == HY - 1 else 2 * s + 1 + d)
                    to_sibling(p)
            for i in ((), (0,), (1, 2), (3, 4))[s]:
                relay_x(i)
        for i in range(NY):
            if i < RELAYED:
                p = from_x(0) * NY + wy(y + order[i])
                for d in range(2):
                    arrived(xg.at[p, :, halves[d]], gx.at[(0, NX - 1)[d], i])
                to_sibling(p)
                continue
            for k in range(NX - 1):
                p = from_x(k) * NY + wy(y + order[i])
                arrived(xg.at[p], gx.at[k, i])
                to_sibling(p)

    def gather_y():
        def piece_of(xx):
            return lambda yy: PER + xx * NY + yy

        streams = [(j, piece_of(xorder[j])) for j in range(NX)]
        for j, piece_at in streams:
            if j:
                end_z(j, za_r.at[j])
                settle(j)
            begin_y(j, piece_at(y), False)
            to_sibling(piece_at(y))
        for s in range(HY):
            for j, piece_at in streams:
                for d in range(2):
                    p = onward_y(j, d, s, piece_at, False)
                    if s < HY - 1 or d == 1:
                        to_sibling(p)

    pl.when(c == 0)(gather_y_then_x)
    pl.when(c == 1)(gather_y)

    def rows_of(a, i):
        return xg[a * PER + i * NY : a * PER + (i + 1) * NY].reshape(ROWS, SL)

    def products(which):
        if which == 0:
            v = dot_nn(rows_of(0, 0), wgu[0, :, own_pair])
            for i in range(1, NX):
                v = v + dot_nn(rows_of(0, i), wgu[i, :, own_pair])
            pre_ref[...] = v
        else:
            v = dot_nt(rows_of(1, 0), wd[0, own_units])
            for i in range(1, NX):
                v = v + dot_nt(rows_of(1, i), wd[i, own_units])
            dh_ref[...] = v

    for when, which in ((0, 0), (1, 1)):
        pl.when(c == when)(functools.partial(products, which))
    arrived(xg.at[pl.ds((1 - c) * PER, PER)], d_recv)
    for when, which in ((0, 1), (1, 0)):
        pl.when(c == when)(functools.partial(products, which))
    pre, d_hidden = pre_ref[...], dh_ref[...]
    gate_pre, up_pre = pre[:, :HID], pre[:, HID:]
    sigma = jax.nn.sigmoid(gate_pre)
    silu = gate_pre * sigma
    hid[:, own_units] = (silu * up_pre).astype(BF16)
    dgu[:, pl.ds(0, HID)] = (d_hidden * up_pre * sigma * (1.0 + gate_pre * (1.0 - sigma))).astype(BF16)
    dgu[:, pl.ds(HID, HID)] = (d_hidden * silu).astype(BF16)

    @pl.when(c == 0)
    def _():
        remote(dgu.at[:, own_pair], dgu.at[:, sib_pair], p_send.at[1], p_recv.at[1], sibling).start()

    @pl.when(c == 1)
    def _():
        remote(hid.at[:, own_units], hid.at[:, sib_units], p_send.at[1], p_recv.at[1], sibling).start()

    def weight_grads(first, last):
        def step(i, carry):
            rows_x = xg[pl.ds(i * NY, NY)].reshape(ROWS, SL)
            rows_g = xg[pl.ds(PER + i * NY, NY)].reshape(ROWS, SL)
            both = dot_tn(rows_x, dgu[:, own_pair])
            span = pl.ds(pl.multiple_of(i * SL, 128), SL)
            gg_ref[span, :] = both[:, :HID].astype(BF16)
            gu_ref[span, :] = both[:, HID:].astype(BF16)
            gd_ref[:, span] = dot_tn(hid[:, own_units], rows_g).astype(BF16)
            return carry

        lax.fori_loop(first, last, step, 0)

    weight_grads(0, NX // 2)

    def expert_out_chunk(j):
        xx = wx(x + 2 - j)
        part[pl.ds(xx * NY, NY)] = dot_nn(hid[...], wd[xx]).reshape(NY, PIECE, SL)

    def input_grad_chunk(j):
        xx = wx(x + 2 - j)
        part[pl.ds(xx * NY, NY)] = dot_nt(dgu[...], wgu[xx]).reshape(NY, PIECE, SL)

    def own(p):
        return part[p]

    def y_out(j, d, s, v):
        out, into = ys.at[j, d, s], yr.at[j, d, s]
        if s == HY - 1:
            out, into = out.at[:, halves[d]], into.at[:, halves[d]]
            v = v[:, :HS] if d == 0 else v[:, HS:]
        out[...] = v.astype(BF16)
        hop = yfar if s == HY - 1 or (s == 1 and c_short[0]) else ynear
        remote(out, into, ry_s.at[j, d, s], ry_r.at[j, d, s], hop[d]).start()

    def y_came(j, d, s):
        into = yr.at[j, d, s]
        if s == HY - 1:
            into = into.at[:, halves[d]]
        arrived(into, ry_r.at[j, d, s])
        return into[...].astype(F32)

    def y_first(j, get):
        for d in range(2):
            y_out(j, d, 2, get(3 - 6 * d))
        v = get(HY)
        for d in range(2):
            y_out(j, d, 3, v)

    def y_second(j, d, get):
        v = get(2 - 4 * d) + y_came(j, d, 2)
        half = y_came(j, d, 3)
        lo, hi = v[:, :HS], v[:, HS:]
        lo, hi = (lo + half, hi) if d == 0 else (lo, hi + half)
        y_out(j, d, 1, jnp.concatenate([lo, hi], axis=1))

    def x_out(k, i, v):
        xs[k, i] = v.astype(BF16)
        remote(xs.at[k, i], xr.at[k, i], rx_s.at[k, i], rx_r.at[k, i], xdev[k]).start()

    def x_came(i):
        v = None
        for k in range(NX - 1):
            arrived(xr.at[k, i], rx_r.at[k, i])
            w = xr[k, i].astype(F32)
            v = w if v is None else v + w
        return v

    c_short = [False]
    back_order = (3, -3, HY, 2, -2, 1, -1, 0)
    chunk_of = (0, 1, 3)
    chunk_order = chunk_of + (2,)

    def at_y(off):
        return wy(y + off)

    def begin_x_then_y():
        arrived(wd.at[:, sib_units], p_recv.at[0])
        arrived(hid.at[:, sib_units], p_recv.at[1])
        for j in chunk_of:
            expert_out_chunk(j)
        for i, off in enumerate(back_order):
            for k in range(NX - 1):
                x_out(k, i, own(wx(x + 2 - chunk_of[k]) * NY + at_y(off)))
        expert_out_chunk(2)

    def begin_y_then_x():
        arrived(wgu.at[:, :, sib_pair], p_recv.at[0])
        arrived(dgu.at[:, sib_pair], p_recv.at[1])
        for j in chunk_order:
            input_grad_chunk(j)
            y_first(j, lambda off: own(wx(x + 2 - j) * NY + at_y(off)))

    pl.when(c == 0)(begin_x_then_y)
    pl.when(c == 1)(begin_y_then_x)

    weight_grads(NX // 2, NX)

    def end_x_then_y():
        c_short[0] = True

        def get(off):
            return own(x * NY + at_y(off)) + x_came(back_order.index(off))

        y_first(0, get)
        for d in range(2):
            y_second(0, d, get)
        for d in range(2):
            y_out(0, d, 0, get(1 - 2 * d))
        v = get(0)
        for s in range(2):
            for d in range(2):
                v = v + y_came(0, d, s)
        res[x] = v

    def end_y_then_x():
        c_short[0] = False

        def get(j):
            return lambda off: own(wx(x + 2 - j) * NY + at_y(off))

        for j in chunk_order:
            for d in range(2):
                y_second(j, d, get(j))
        for j in chunk_order:
            for d in range(2):
                y_out(j, d, 0, get(j)(1 - 2 * d) + y_came(j, d, 1))
        for j in chunk_order:
            v = get(j)(0) + y_came(j, 0, 0) + y_came(j, 1, 0)
            if j in chunk_of:
                x_out(chunk_of.index(j), 0, v)
            else:
                res[x] = v
        res[x] = res[x] + x_came(0)

    pl.when(c == 0)(end_x_then_y)
    pl.when(c == 1)(end_y_then_x)

    done = res[x].astype(BF16)
    back = (dot_tn(tidy0, done[:, :HS]) + dot_tn(tidy1, done[:, HS:])).astype(BF16)
    for e in range(NZ):
        slab_out[NX, e] = back[e * 16 : (e + 1) * 16]
    slab_in[NX, z] = slab_out[NX, z]
    start_z(NX, zb_s, zb_r)
    end_z(NX, zb_r)
    chosen = dot_nn(pick[...], slab_in[NX].reshape(NZ * 16, HS))
    c0 = jnp.where(c == 0, cw0, one)
    c1 = jnp.where(c == 0, cw1, one)
    scores = [jnp.zeros((TOKB, 1), F32), jnp.zeros((TOKB, 1), F32)]
    load_go.wait()
    for h, span in enumerate(spans):
        first = chosen[2 * h * TOKB : (2 * h + 1) * TOKB]
        second = chosen[(2 * h + 1) * TOKB : (2 * h + 2) * TOKB]
        fin[tp, :, h * HS : (h + 1) * HS] = (c0 * first + c1 * second).astype(BF16)
        g = gos[:, span].astype(F32)
        scores[0] = scores[0] + jnp.sum(g * first, axis=1, keepdims=True)
        scores[1] = scores[1] + jnp.sum(g * second, axis=1, keepdims=True)
    lane = lax.broadcasted_iota(jnp.int32, (TOKB, 128), 1)
    fsc[tp] = jnp.where(lane == 0, scores[0], jnp.where(lane == 1, scores[1], 0.0))

    for d in [NT // 2] + [d for k in range(NT // 2 - 1, 0, -1) for d in (k, NT - k)]:
        remote(fin.at[tp], fin.at[tp], f_s.at[0, d], f_r.at[0, d], peers_t[d - 1]).start()
        remote(fsc.at[tp], fsc.at[tp], f_s.at[1, d], f_r.at[1, d], peers_t[d - 1]).start()
    for d in range(1, NT):
        source = lax.rem(tp - d + NT, NT)
        arrived(fin.at[source], f_r.at[0, d])
        arrived(fsc.at[source], f_r.at[1, d])
    total_score = fsc[0]
    for i in range(NX):
        mixed_ref[:, i * SL : (i + 1) * SL] = fin[CORES * i]
        gtok_ref[:, i * SL : (i + 1) * SL] = fin[CORES * i + 1]
        if i:
            total_score = total_score + fsc[CORES * i]
    for k in range(2):
        gcomb_ref[k : k + 1, :] = jnp.sum(jnp.where(diagonal, total_score[:, k : k + 1], 0.0), axis=0, keepdims=True)

    for d in range(1, NZ):
        sent(slab_out.at[0, 0], za_s.at[0, d])
        sent(slab_out.at[0, 0], zb_s.at[d])
    for d in range(1, NT):
        sent(fin.at[tp], f_s.at[0, d])
        sent(fsc.at[tp], f_s.at[1, d])
    sent(xg.at[pl.ds(c * PER, PER)], d_send)

    def y_sent(j):
        for d in range(2):
            sent(ys.at[j, d, HY - 1].at[:, halves[d]], ry_s.at[j, d, HY - 1])
            for t in range(HY - 1):
                sent(ys.at[j, d, t], ry_s.at[j, d, t])

    @pl.when(c == 0)
    def _():
        sent(xg.at[pl.ds(0, PER - 1)], g_send)
        sent(wgu.at[:, :, own_pair], p_send.at[0])
        sent(dgu.at[:, own_pair], p_send.at[1])
        for k in range(NX - 1):
            for i in range(NY):
                sent(xs.at[k, i], rx_s.at[k, i])
        y_sent(0)

    @pl.when(c == 1)
    def _():
        sent(xg.at[pl.ds(0, PER - NX)], g_send)
        for j in range(1, NX):
            for d in range(1, NZ):
                sent(slab_out.at[0, 0], za_s.at[j, d])
        sent(wd.at[:, own_units], p_send.at[0])
        sent(hid.at[:, own_units], p_send.at[1])
        for k in range(NX - 1):
            sent(xs.at[k, 0], rx_s.at[k, 0])
        for j in range(NX):
            y_sent(j)


def flush(*refs):
    n = len(refs) // 2
    sems = refs[-1]
    copies = [pltpu.make_async_copy(refs[i], refs[n + i], sems.at[i]) for i in range(n)]
    for copy in copies:
        copy.start()
    for copy in copies:
        copy.wait()


def solution(mesh, cap=CAP, planes=8):
    NT = mesh.shape["tp"]
    NX, NZ = NT // CORES, planes
    NY = mesh.shape["ep"] // NZ

    def step(tokens, expert_ids, combine, grad_out, gate_weight, up_weight, down_weight):
        tokb, d = tokens.shape
        hidden = gate_weight.shape[1]
        sl, piece, per = d // NX, NZ * cap, NX * NY
        hs, rows, half_y = sl // 2, NY * piece, NY // 2
        dma, vmem, hbm = pltpu.SemaphoreType.DMA, pltpu.VMEM, pl.BlockSpec(memory_space=pl.ANY)
        held = pl.BlockSpec(memory_space=pltpu.VMEM)
        mixed, gtok, gcomb, gg, gu, gd = pl.pallas_call(
            functools.partial(kernel, (NX, NY, NZ, cap)),
            out_shape=(
                vmem((tokb, d), BF16),
                vmem((tokb, d), BF16),
                vmem(combine.shape[::-1], F32),
                vmem(gate_weight.shape, BF16),
                vmem(up_weight.shape, BF16),
                vmem(down_weight.shape, BF16),
            ),
            in_specs=[held] * 2 + [hbm] * 5,
            out_specs=[held] * 6,
            scratch_shapes=[
                vmem((2 * per, piece, sl), BF16),
                vmem((per, piece, sl), F32),
                vmem((NX - 1, NY, piece, sl), BF16),
                vmem((NX - 1, NY, piece, sl), BF16),
                vmem((NX, 2, half_y, piece, sl), BF16),
                vmem((NX, 2, half_y, piece, sl), BF16),
                vmem((NX, piece, sl), F32),
                vmem((NX + 1, NZ, 16, hs), BF16),
                vmem((NX + 1, NZ, 16, hs), BF16),
                vmem((NT, tokb, sl), BF16),
                vmem((NT, tokb, 128), F32),
                vmem((4 * tokb, NZ * 16), BF16),
                vmem((tokb, d), BF16), vmem((tokb, sl), BF16),
                vmem((NX, sl, 4 * hidden), BF16),
                vmem((NX, 2 * hidden, sl), BF16),
                vmem((rows, 2 * hidden), BF16),
                vmem((rows, 4 * hidden), BF16),
                vmem((rows, 2 * hidden), F32), vmem((rows, hidden), F32),
                dma((3 * NX,)), dma((2,)),
                dma((NX, NZ)), dma((NX, NZ)), dma((NZ,)), dma((NZ,)),
                dma((NX, NY)), dma((NX, 2, half_y)),
                dma(()), dma(()), dma(()),
                dma((2,)), dma((2,)),
                dma((NX - 1, NY)), dma((NX - 1, NY)),
                dma((NX, 2, half_y)), dma((NX, 2, half_y)),
                dma((2, NT)), dma((2, NT)),
            ],
            compiler_params=pltpu.CompilerParams(
                collective_id=0, has_side_effects=True, vmem_limit_bytes=56 * 2**20
            ),
        )(expert_ids.T, combine.T, tokens, grad_out, gate_weight, up_weight, down_weight)
        made = (gg, gu, gd, mixed, gtok, gcomb)
        gg, gu, gd, mixed, gtok, gcomb = pl.pallas_call(
            flush,
            out_shape=tuple(jax.ShapeDtypeStruct(m.shape, m.dtype) for m in made),
            in_specs=[held] * len(made),
            out_specs=[hbm] * len(made),
            scratch_shapes=[dma((len(made),))],
        )(*[pltpu.with_memory_space_constraint(m, pltpu.VMEM) for m in made])
        return mixed, gtok, gcomb.T, gg, gu, gd

    return jax.shard_map(
        step,
        mesh=mesh,
        in_specs=(
            P("ep", None),
            P("ep", None),
            P("ep", None),
            P("ep", None),
            P(None, ("ep", "tp")),
            P(None, ("ep", "tp")),
            P(("ep", "tp"), None),
        ),
        out_specs=(
            P("ep", None),
            P("ep", None),
            P("ep", None),
            P(None, ("ep", "tp")),
            P(None, ("ep", "tp")),
            P(("ep", "tp"), None),
        ),
        check_vma=False,
    )
```

```python
import functools

import jax
import jax.numpy as jnp
from jax import lax
from jax.experimental import pallas as pl
from jax.experimental.pallas import tpu as pltpu
from jax.sharding import PartitionSpec as P

CAP = 6
CORES = 2
MESH = pl.DeviceIdType.MESH
F32 = jnp.float32
BF16 = jnp.bfloat16


def dot_nn(a, b):
    return jnp.dot(a, b, preferred_element_type=F32)


def dot_nt(a, b):
    return lax.dot_general(a, b, (((1,), (1,)), ((), ())), preferred_element_type=F32)


def dot_tn(a, b):
    return lax.dot_general(a, b, (((0,), (0,)), ((), ())), preferred_element_type=F32)


def kernel(
    dims,
    ids_ref, comb_ref, tok_hbm, go_hbm, gate_hbm, up_hbm, down_hbm,
    mixed_ref, gtok_ref, gcomb_ref, gg_ref, gu_ref, gd_ref,
    xg, part, xs, xr, ys, yr, res,
    slab_out, slab_in, fin, fsc, pick, src, gos, wgu, wd, hid, dgu, pre_ref, dh_ref,
    w_sem, t_sem, za_s, za_r, zb_s, zb_r, gx, gy, g_send, d_send, d_recv,
    p_send, p_recv, rx_s, rx_r, ry_s, ry_r, f_s, f_r,
):
    NX, NY, NZ, CAPA = dims
    PIECE = NZ * CAPA
    TOKB, D = tok_hbm.shape
    SL = D // NX
    HS = SL // 2
    ROWS = NY * PIECE
    PER = NX * NY
    HID = wd.shape[1] // 2

    ep, tp = lax.axis_index("ep"), lax.axis_index("tp")
    c, x = lax.rem(tp, CORES), lax.div(tp, CORES)
    y, z = lax.rem(ep, NY), lax.div(ep, NY)

    def wx(v):
        return lax.rem(v + 2 * NX, NX)

    def wy(v):
        return lax.rem(v + 2 * NY, NY)

    def at(xx, yy, zz, cc):
        return (zz * NY + yy, xx * CORES + cc)

    yup, ydown = at(x, wy(y + 1), z, c), at(x, wy(y - 1), z, c)
    sibling = at(x, y, z, 1 - c)

    def remote(src, dst, ssem, rsem, device):
        return pltpu.make_async_remote_copy(
            src_ref=src, dst_ref=dst, send_sem=ssem, recv_sem=rsem,
            device_id=device, device_id_type=MESH,
        )

    def arrived(dst, rsem):
        remote(dst, dst, rsem, rsem, sibling).wait_recv()

    def sent(src, ssem):
        remote(src, src, ssem, ssem, sibling).wait_send()

    barrier = pltpu.get_barrier_semaphore()
    peers_z = [at(x, y, lax.rem(z + d, NZ), c) for d in range(1, NZ)]
    NT = NX * CORES
    peers_t = [(ep, lax.rem(tp + d, NT)) for d in range(1, NT)]
    far_up, far_down = at(x, wy(y + 2), z, c), at(x, wy(y - 2), z, c)
    partners = peers_z + peers_t + [yup, ydown, far_up, far_down]
    ynear, yfar = (yup, ydown), (far_up, far_down)
    xdev = [at(wx(x + k), y, z, c) for k in (2, 1, NX - 1)]
    for device in partners:
        pl.semaphore_signal(barrier, inc=1, device_id=device, device_id_type=MESH)

    features = pl.ds(pl.multiple_of(x * SL, 128), SL)

    @pl.when(c == 0)
    def _():
        pltpu.make_async_copy(tok_hbm, src, t_sem.at[0]).start()

    @pl.when(c == 1)
    def _():
        pltpu.make_async_copy(go_hbm, src, t_sem.at[0]).start()

    load_go = pltpu.make_async_copy(go_hbm.at[:, features], gos, t_sem.at[1])
    load_go.start()
    own_units, sib_units = (pl.ds(0, HID), pl.ds(HID, HID))
    own_pair, sib_pair = (pl.ds(0, 2 * HID), pl.ds(2 * HID, 2 * HID))
    loads = []
    for i in range(NX):
        rows = pl.ds(i * SL, SL)
        loads.append(pltpu.make_async_copy(gate_hbm.at[rows, :], wgu.at[i, :, pl.ds(0, HID)], w_sem.at[3 * i]))
        loads.append(pltpu.make_async_copy(up_hbm.at[rows, :], wgu.at[i, :, pl.ds(HID, HID)], w_sem.at[3 * i + 1]))
        loads.append(pltpu.make_async_copy(down_hbm.at[:, rows], wd.at[i, own_units], w_sem.at[3 * i + 2]))
    for load in loads:
        load.start()

    lane = lax.broadcasted_iota(jnp.int32, (TOKB, NZ * 16), 1)
    expert, place = lax.shift_right_logical(lane, 4), lane & 15
    diagonal = lax.broadcasted_iota(jnp.int32, (TOKB, TOKB), 0) == lax.broadcasted_iota(jnp.int32, (TOKB, TOKB), 1)

    def column(ref, k):
        return jnp.sum(jnp.where(diagonal, ref[k : k + 1, :].astype(F32), 0.0), axis=1, keepdims=True)

    id0, id1 = column(ids_ref, 0).astype(jnp.int32), column(ids_ref, 1).astype(jnp.int32)
    cw0, cw1 = column(comb_ref, 0), column(comb_ref, 1)
    is0, is1 = id0 == expert, id1 == expert
    named = jnp.where(is0 | is1, 1.0, 0.0)
    earlier = jnp.where(
        lax.broadcasted_iota(jnp.int32, (TOKB, TOKB), 0) > lax.broadcasted_iota(jnp.int32, (TOKB, TOKB), 1), 1.0, 0.0
    )
    rank = dot_nn(earlier.astype(BF16), named.astype(BF16)).astype(jnp.int32)
    hit0 = rank == place
    hit1 = (rank + CAPA == place) & (rank < CAPA)
    hit0 = hit0 & (place < CAPA)
    for g, mask in enumerate((is0 & hit0, is1 & hit0, is0 & hit1, is1 & hit1)):
        pick[g * TOKB : (g + 1) * TOKB, :] = jnp.where(mask, 1.0, 0.0).astype(BF16)

    one = jnp.ones((TOKB, 1), F32)
    w0 = jnp.where(c == 0, one, cw0)
    w1 = jnp.where(c == 0, one, cw1)
    spans = (slice(0, HS), slice(HS, SL))
    pltpu.make_async_copy(go_hbm, src, t_sem.at[0]).wait()
    far_first = [NZ // 2] + [d for k in range(NZ // 2 - 1, 0, -1) for d in (k, NZ - k)]
    xorder = [x, wx(x - 1), wx(x + 1), wx(x + 2)]

    def make_slabs(j):
        sources = []
        for h in range(2):
            span = pl.ds(pl.multiple_of(xorder[j] * SL + h * HS, 128), HS)
            v = src[:, span].astype(F32)
            sources += [(v * w0).astype(BF16), (v * w1).astype(BF16)]
        slabs = dot_tn(pick[...], jnp.concatenate(sources, axis=0)).astype(BF16)
        for e in range(NZ):
            slab_out[j, e] = slabs[e * 16 : (e + 1) * 16]
        slab_in[j, z] = slab_out[j, z]

    make_slabs(0)

    pl.semaphore_wait(barrier, len(partners))

    def give_weights():
        for load in loads:
            load.wait()

        @pl.when(c == 0)
        def _():
            remote(wgu.at[:, :, own_pair], wgu.at[:, :, sib_pair], p_send.at[0], p_recv.at[0], sibling).start()

        @pl.when(c == 1)
        def _():
            remote(wd.at[:, own_units], wd.at[:, sib_units], p_send.at[0], p_recv.at[0], sibling).start()

    def start_z(which, s_sem, r_sem):
        for d in far_first:
            remote(
                slab_out.at[which, lax.rem(z + d, NZ)], slab_in.at[which, z],
                s_sem.at[d], r_sem.at[d], peers_z[d - 1],
            ).start()

    def end_z(which, r_sem):
        for d in range(1, NZ):
            arrived(slab_in.at[which, lax.rem(z - d + NZ, NZ)], r_sem.at[d])

    start_z(0, za_s.at[0], za_r.at[0])

    @pl.when(c == 1)
    def _():
        for j in range(1, NX):
            make_slabs(j)
            start_z(j, za_s.at[j], za_r.at[j])

    give_weights()
    end_z(0, za_r.at[0])

    row = lax.broadcasted_iota(jnp.int32, (PIECE, NZ * 16), 0)
    col = lax.broadcasted_iota(jnp.int32, (PIECE, NZ * 16), 1)
    block, inner = lax.shift_right_logical(col, 4), col & 15
    tidy0 = jnp.where((block * CAPA + inner == row) & (inner < CAPA), 1.0, 0.0).astype(BF16)
    tidy1 = jnp.where(
        (block * CAPA + inner - CAPA == row) & (inner >= CAPA) & (inner < 2 * CAPA), 1.0, 0.0
    ).astype(BF16)

    def settle(j):
        got = slab_in[j].reshape(NZ * 16, HS)
        mine = c * PER + xorder[j] * NY + y
        xg[mine, :, 0:HS] = dot_nn(tidy0, got).astype(BF16)
        xg[mine, :, HS:SL] = dot_nn(tidy1, got).astype(BF16)

    settle(0)

    halves = (pl.ds(0, HS), pl.ds(HS, HS))
    HY = NY // 2
    order = (0, -1, 1, -2, 2, -3, 3, HY)

    def to_sibling(p):
        remote(xg.at[p], xg.at[p], d_send, d_recv, sibling).start()

    def send(ref, sem, device):
        remote(ref, ref, g_send, sem, device).start()

    def along_x(p, i):
        for k in range(NX - 1):
            send(xg.at[p], gx.at[k, i], xdev[k])

    def from_x(k):
        return wx(x - (2, 1, -1)[k])

    def begin_y(j, p, short):
        for d in range(2):
            if short:
                send(xg.at[p], gy.at[j, d, 1], yfar[d])
            send(xg.at[p], gy.at[j, d, 0], ynear[d])

    def onward_y(j, d, s, piece_at, short):
        p = piece_at(wy(y - s - 1 if d == 0 else y + s + 1))
        if s == HY - 1:
            arrived(xg.at[p, :, halves[d]], gy.at[j, d, s])
            return p
        arrived(xg.at[p], gy.at[j, d, s])
        if s == 0 and not short:
            send(xg.at[p], gy.at[j, d, 1], ynear[d])
        chain = not short
        if s == 1:
            send(xg.at[p], gy.at[j, d, 2], ynear[d])
        if s == (2 if chain else 1):
            send(xg.at[p, :, halves[d]], gy.at[j, d, 3], ynear[d] if chain else yfar[d])
        return p

    def gather_y_then_x():
        def piece_at(yy):
            return x * NY + yy

        p = piece_at(y)
        begin_y(0, p, True)
        along_x(p, 0)
        to_sibling(p)
        for s in range(HY):
            for d in range(2):
                p = onward_y(0, d, s, piece_at, True)
                if s < HY - 1 or d == 1:
                    along_x(p, 2 * s + 1 if s == HY - 1 else 2 * s + 1 + d)
                    to_sibling(p)
        for i in range(NY):
            for k in range(NX - 1):
                p = from_x(k) * NY + wy(y + order[i])
                arrived(xg.at[p], gx.at[k, i])
                to_sibling(p)

    def gather_y():
        def piece_of(xx):
            return lambda yy: PER + xx * NY + yy

        streams = [(j, piece_of(xorder[j])) for j in range(NX)]
        for j, piece_at in streams:
            if j:
                end_z(j, za_r.at[j])
                settle(j)
            begin_y(j, piece_at(y), False)
            to_sibling(piece_at(y))
        for s in range(HY):
            for j, piece_at in streams:
                for d in range(2):
                    p = onward_y(j, d, s, piece_at, False)
                    if s < HY - 1 or d == 1:
                        to_sibling(p)

    pl.when(c == 0)(gather_y_then_x)
    pl.when(c == 1)(gather_y)

    def rows_of(a, i):
        return xg[a * PER + i * NY : a * PER + (i + 1) * NY].reshape(ROWS, SL)

    def products(which):
        if which == 0:
            v = dot_nn(rows_of(0, 0), wgu[0, :, own_pair])
            for i in range(1, NX):
                v = v + dot_nn(rows_of(0, i), wgu[i, :, own_pair])
            pre_ref[...] = v
        else:
            v = dot_nt(rows_of(1, 0), wd[0, own_units])
            for i in range(1, NX):
                v = v + dot_nt(rows_of(1, i), wd[i, own_units])
            dh_ref[...] = v

    for when, which in ((0, 0), (1, 1)):
        pl.when(c == when)(functools.partial(products, which))
    arrived(xg.at[pl.ds((1 - c) * PER, PER)], d_recv)
    for when, which in ((0, 1), (1, 0)):
        pl.when(c == when)(functools.partial(products, which))
    pre, d_hidden = pre_ref[...], dh_ref[...]
    gate_pre, up_pre = pre[:, :HID], pre[:, HID:]
    sigma = jax.nn.sigmoid(gate_pre)
    silu = gate_pre * sigma
    hid[:, own_units] = (silu * up_pre).astype(BF16)
    dgu[:, pl.ds(0, HID)] = (d_hidden * up_pre * sigma * (1.0 + gate_pre * (1.0 - sigma))).astype(BF16)
    dgu[:, pl.ds(HID, HID)] = (d_hidden * silu).astype(BF16)

    @pl.when(c == 0)
    def _():
        remote(dgu.at[:, own_pair], dgu.at[:, sib_pair], p_send.at[1], p_recv.at[1], sibling).start()

    @pl.when(c == 1)
    def _():
        remote(hid.at[:, own_units], hid.at[:, sib_units], p_send.at[1], p_recv.at[1], sibling).start()

    def weight_grads(first, last):
        def step(i, carry):
            rows_x = xg[pl.ds(i * NY, NY)].reshape(ROWS, SL)
            rows_g = xg[pl.ds(PER + i * NY, NY)].reshape(ROWS, SL)
            both = dot_tn(rows_x, dgu[:, own_pair])
            span = pl.ds(pl.multiple_of(i * SL, 128), SL)
            gg_ref[span, :] = both[:, :HID].astype(BF16)
            gu_ref[span, :] = both[:, HID:].astype(BF16)
            gd_ref[:, span] = dot_tn(hid[:, own_units], rows_g).astype(BF16)
            return carry

        lax.fori_loop(first, last, step, 0)

    weight_grads(0, NX // 2)

    def expert_out_chunk(j):
        xx = wx(x + 2 - j)
        part[pl.ds(xx * NY, NY)] = dot_nn(hid[...], wd[xx]).reshape(NY, PIECE, SL)

    def input_grad_chunk(j):
        xx = wx(x + 2 - j)
        part[pl.ds(xx * NY, NY)] = dot_nt(dgu[...], wgu[xx]).reshape(NY, PIECE, SL)

    def own(p):
        return part[p]

    def y_out(j, d, s, v):
        out, into = ys.at[j, d, s], yr.at[j, d, s]
        if s == HY - 1:
            out, into = out.at[:, halves[d]], into.at[:, halves[d]]
            v = v[:, :HS] if d == 0 else v[:, HS:]
        out[...] = v.astype(BF16)
        hop = yfar if s == HY - 1 or (s == 1 and c_short[0]) else ynear
        remote(out, into, ry_s.at[j, d, s], ry_r.at[j, d, s], hop[d]).start()

    def y_came(j, d, s):
        into = yr.at[j, d, s]
        if s == HY - 1:
            into = into.at[:, halves[d]]
        arrived(into, ry_r.at[j, d, s])
        return into[...].astype(F32)

    def y_first(j, get):
        for d in range(2):
            y_out(j, d, 2, get(3 - 6 * d))
        v = get(HY)
        for d in range(2):
            y_out(j, d, 3, v)

    def y_second(j, d, get):
        v = get(2 - 4 * d) + y_came(j, d, 2)
        half = y_came(j, d, 3)
        lo, hi = v[:, :HS], v[:, HS:]
        lo, hi = (lo + half, hi) if d == 0 else (lo, hi + half)
        y_out(j, d, 1, jnp.concatenate([lo, hi], axis=1))

    def x_out(k, i, v):
        xs[k, i] = v.astype(BF16)
        remote(xs.at[k, i], xr.at[k, i], rx_s.at[k, i], rx_r.at[k, i], xdev[k]).start()

    def x_came(i):
        v = None
        for k in range(NX - 1):
            arrived(xr.at[k, i], rx_r.at[k, i])
            w = xr[k, i].astype(F32)
            v = w if v is None else v + w
        return v

    c_short = [False]
    back_order = (3, -3, HY, 2, -2, 1, -1, 0)
    chunk_of = (0, 1, 3)
    chunk_order = chunk_of + (2,)

    def at_y(off):
        return wy(y + off)

    def begin_x_then_y():
        arrived(wd.at[:, sib_units], p_recv.at[0])
        arrived(hid.at[:, sib_units], p_recv.at[1])
        for j in chunk_of:
            expert_out_chunk(j)
        for i, off in enumerate(back_order):
            for k in range(NX - 1):
                x_out(k, i, own(wx(x + 2 - chunk_of[k]) * NY + at_y(off)))
        expert_out_chunk(2)

    def begin_y_then_x():
        arrived(wgu.at[:, :, sib_pair], p_recv.at[0])
        arrived(dgu.at[:, sib_pair], p_recv.at[1])
        for j in chunk_order:
            input_grad_chunk(j)
            y_first(j, lambda off: own(wx(x + 2 - j) * NY + at_y(off)))

    pl.when(c == 0)(begin_x_then_y)
    pl.when(c == 1)(begin_y_then_x)

    weight_grads(NX // 2, NX)

    def end_x_then_y():
        c_short[0] = True

        def get(off):
            return own(x * NY + at_y(off)) + x_came(back_order.index(off))

        y_first(0, get)
        for d in range(2):
            y_second(0, d, get)
        for d in range(2):
            y_out(0, d, 0, get(1 - 2 * d))
        v = get(0)
        for s in range(2):
            for d in range(2):
                v = v + y_came(0, d, s)
        res[x] = v

    def end_y_then_x():
        c_short[0] = False

        def get(j):
            return lambda off: own(wx(x + 2 - j) * NY + at_y(off))

        for j in chunk_order:
            for d in range(2):
                y_second(j, d, get(j))
        for j in chunk_order:
            for d in range(2):
                y_out(j, d, 0, get(j)(1 - 2 * d) + y_came(j, d, 1))
        for j in chunk_order:
            v = get(j)(0) + y_came(j, 0, 0) + y_came(j, 1, 0)
            if j in chunk_of:
                x_out(chunk_of.index(j), 0, v)
            else:
                res[x] = v
        res[x] = res[x] + x_came(0)

    pl.when(c == 0)(end_x_then_y)
    pl.when(c == 1)(end_y_then_x)

    done = res[x].astype(BF16)
    back = (dot_tn(tidy0, done[:, :HS]) + dot_tn(tidy1, done[:, HS:])).astype(BF16)
    for e in range(NZ):
        slab_out[NX, e] = back[e * 16 : (e + 1) * 16]
    slab_in[NX, z] = slab_out[NX, z]
    start_z(NX, zb_s, zb_r)
    end_z(NX, zb_r)
    chosen = dot_nn(pick[...], slab_in[NX].reshape(NZ * 16, HS))
    c0 = jnp.where(c == 0, cw0, one)
    c1 = jnp.where(c == 0, cw1, one)
    scores = [jnp.zeros((TOKB, 1), F32), jnp.zeros((TOKB, 1), F32)]
    load_go.wait()
    for h, span in enumerate(spans):
        first = chosen[2 * h * TOKB : (2 * h + 1) * TOKB]
        second = chosen[(2 * h + 1) * TOKB : (2 * h + 2) * TOKB]
        fin[tp, :, h * HS : (h + 1) * HS] = (c0 * first + c1 * second).astype(BF16)
        g = gos[:, span].astype(F32)
        scores[0] = scores[0] + jnp.sum(g * first, axis=1, keepdims=True)
        scores[1] = scores[1] + jnp.sum(g * second, axis=1, keepdims=True)
    lane = lax.broadcasted_iota(jnp.int32, (TOKB, 128), 1)
    fsc[tp] = jnp.where(lane == 0, scores[0], jnp.where(lane == 1, scores[1], 0.0))

    for d in [NT // 2] + [d for k in range(NT // 2 - 1, 0, -1) for d in (k, NT - k)]:
        remote(fin.at[tp], fin.at[tp], f_s.at[0, d], f_r.at[0, d], peers_t[d - 1]).start()
        remote(fsc.at[tp], fsc.at[tp], f_s.at[1, d], f_r.at[1, d], peers_t[d - 1]).start()
    for d in range(1, NT):
        source = lax.rem(tp - d + NT, NT)
        arrived(fin.at[source], f_r.at[0, d])
        arrived(fsc.at[source], f_r.at[1, d])
    total_score = fsc[0]
    for i in range(NX):
        mixed_ref[:, i * SL : (i + 1) * SL] = fin[CORES * i]
        gtok_ref[:, i * SL : (i + 1) * SL] = fin[CORES * i + 1]
        if i:
            total_score = total_score + fsc[CORES * i]
    for k in range(2):
        gcomb_ref[k : k + 1, :] = jnp.sum(jnp.where(diagonal, total_score[:, k : k + 1], 0.0), axis=0, keepdims=True)

    for d in range(1, NZ):
        sent(slab_out.at[0, 0], za_s.at[0, d])
        sent(slab_out.at[0, 0], zb_s.at[d])
    for d in range(1, NT):
        sent(fin.at[tp], f_s.at[0, d])
        sent(fsc.at[tp], f_s.at[1, d])
    sent(xg.at[pl.ds(c * PER, PER)], d_send)

    def y_sent(j):
        for d in range(2):
            sent(ys.at[j, d, HY - 1].at[:, halves[d]], ry_s.at[j, d, HY - 1])
            for t in range(HY - 1):
                sent(ys.at[j, d, t], ry_s.at[j, d, t])

    @pl.when(c == 0)
    def _():
        sent(xg.at[pl.ds(0, PER - 1)], g_send)
        sent(wgu.at[:, :, own_pair], p_send.at[0])
        sent(dgu.at[:, own_pair], p_send.at[1])
        for k in range(NX - 1):
            for i in range(NY):
                sent(xs.at[k, i], rx_s.at[k, i])
        y_sent(0)

    @pl.when(c == 1)
    def _():
        sent(xg.at[pl.ds(0, PER - NX)], g_send)
        for j in range(1, NX):
            for d in range(1, NZ):
                sent(slab_out.at[0, 0], za_s.at[j, d])
        sent(wd.at[:, own_units], p_send.at[0])
        sent(hid.at[:, own_units], p_send.at[1])
        for k in range(NX - 1):
            sent(xs.at[k, 0], rx_s.at[k, 0])
        for j in range(NX):
            y_sent(j)


def flush(*refs):
    n = len(refs) // 2
    sems = refs[-1]
    copies = [pltpu.make_async_copy(refs[i], refs[n + i], sems.at[i]) for i in range(n)]
    for copy in copies:
        copy.start()
    for copy in copies:
        copy.wait()


def solution(mesh, cap=CAP, planes=8):
    NT = mesh.shape["tp"]
    NX, NZ = NT // CORES, planes
    NY = mesh.shape["ep"] // NZ

    def step(tokens, expert_ids, combine, grad_out, gate_weight, up_weight, down_weight):
        tokb, d = tokens.shape
        hidden = gate_weight.shape[1]
        sl, piece, per = d // NX, NZ * cap, NX * NY
        hs, rows, half_y = sl // 2, NY * piece, NY // 2
        dma, vmem, hbm = pltpu.SemaphoreType.DMA, pltpu.VMEM, pl.BlockSpec(memory_space=pl.ANY)
        held = pl.BlockSpec(memory_space=pltpu.VMEM)
        mixed, gtok, gcomb, gg, gu, gd = pl.pallas_call(
            functools.partial(kernel, (NX, NY, NZ, cap)),
            out_shape=(
                vmem((tokb, d), BF16),
                vmem((tokb, d), BF16),
                vmem(combine.shape[::-1], F32),
                vmem(gate_weight.shape, BF16),
                vmem(up_weight.shape, BF16),
                vmem(down_weight.shape, BF16),
            ),
            in_specs=[held] * 2 + [hbm] * 5,
            out_specs=[held] * 6,
            scratch_shapes=[
                vmem((2 * per, piece, sl), BF16),
                vmem((per, piece, sl), F32),
                vmem((NX - 1, NY, piece, sl), BF16),
                vmem((NX - 1, NY, piece, sl), BF16),
                vmem((NX, 2, half_y, piece, sl), BF16),
                vmem((NX, 2, half_y, piece, sl), BF16),
                vmem((NX, piece, sl), F32),
                vmem((NX + 1, NZ, 16, hs), BF16),
                vmem((NX + 1, NZ, 16, hs), BF16),
                vmem((NT, tokb, sl), BF16),
                vmem((NT, tokb, 128), F32),
                vmem((4 * tokb, NZ * 16), BF16),
                vmem((tokb, d), BF16), vmem((tokb, sl), BF16),
                vmem((NX, sl, 4 * hidden), BF16),
                vmem((NX, 2 * hidden, sl), BF16),
                vmem((rows, 2 * hidden), BF16),
                vmem((rows, 4 * hidden), BF16),
                vmem((rows, 2 * hidden), F32), vmem((rows, hidden), F32),
                dma((3 * NX,)), dma((2,)),
                dma((NX, NZ)), dma((NX, NZ)), dma((NZ,)), dma((NZ,)),
                dma((NX - 1, NY)), dma((NX, 2, half_y)),
                dma(()), dma(()), dma(()),
                dma((2,)), dma((2,)),
                dma((NX - 1, NY)), dma((NX - 1, NY)),
                dma((NX, 2, half_y)), dma((NX, 2, half_y)),
                dma((2, NT)), dma((2, NT)),
            ],
            compiler_params=pltpu.CompilerParams(
                collective_id=0, has_side_effects=True, vmem_limit_bytes=56 * 2**20
            ),
        )(expert_ids.T, combine.T, tokens, grad_out, gate_weight, up_weight, down_weight)
        made = (gg, gu, gd, mixed, gtok, gcomb)
        gg, gu, gd, mixed, gtok, gcomb = pl.pallas_call(
            flush,
            out_shape=tuple(jax.ShapeDtypeStruct(m.shape, m.dtype) for m in made),
            in_specs=[held] * len(made),
            out_specs=[hbm] * len(made),
            scratch_shapes=[dma((len(made),))],
        )(*[pltpu.with_memory_space_constraint(m, pltpu.VMEM) for m in made])
        return mixed, gtok, gcomb.T, gg, gu, gd

    return jax.shard_map(
        step,
        mesh=mesh,
        in_specs=(
            P("ep", None),
            P("ep", None),
            P("ep", None),
            P("ep", None),
            P(None, ("ep", "tp")),
            P(None, ("ep", "tp")),
            P(("ep", "tp"), None),
        ),
        out_specs=(
            P("ep", None),
            P("ep", None),
            P("ep", None),
            P(None, ("ep", "tp")),
            P(None, ("ep", "tp")),
            P(("ep", "tp"), None),
        ),
        check_vma=False,
    )
```
